32 devices in a mesh: gx: 8 (over z, y), gy: 4 (over x, core).
Axes of the slice: x: 2, y: 2, z: 4, core: 2. Of those that a mesh axis runs over, the one named last changes fastest.
Arguments:
- efield: float32 [3, 128, 128, 128], P(None, 'gx', 'gy'), may hold values from -6 to 6
- hfield: float32 [3, 128, 128, 128], P(None, 'gx', 'gy'), may hold values from -6 to 6
- polar: float32 [3, 128, 128, 128], P(None, 'gx', 'gy'), may hold values from -6 to 6
- material_map: int32 [128, 128, 128], P('gx', 'gy'), may hold values from 0 to 2
- via_index: int32 [128, 128, 128], P('gx', 'gy'), may hold values from 0 to 7
- fill_fraction: float32 [128, 128, 128], P('gx', 'gy'), may hold values from 0 to 1
- permittivity: float32 [3], replicated, may hold values from 1 to 5
- conductivity: float32 [3], replicated, may hold values from 0 to 2
- debye_strength: float32 [3], replicated, may hold values from 0.5 to 3
- relax_time: float32 [3], replicated, may hold values from 0.5 to 5
- conformal: float32 [8, 3], replicated, may hold values from 0.3 to 1
Outputs:
- efield_out: float32 [3, 128, 128, 128], P(None, 'gx', 'gy')
- hfield_out: float32 [3, 128, 128, 128], P(None, 'gx', 'gy')
- polar_out: float32 [3, 128, 128, 128], P(None, 'gx', 'gy')
The draws below stay inside these ranges and needn't reach their ends.
Inputs may be any that keep to these rules, and one draw needn't show every extreme that they name: `via_index`: a row of the conformal table.
All inputs are finite; a program needn't handle non-finite values.
Results may differ from the reference program's by a relative error of at most 0.00002.
Values sent between devices are 32-bit elements; how exact they have to be, the bound alone decides.
A program may use at most 64 MiB of HBM per device.

```python
import math
import jax
import jax.numpy as jnp
from jax import lax

NZ = 128
STEPS = 4
NMAT = 3
VIAS = 8
NX = 128
NY = 128


def touch_ends(values, stream_key, least, high):
    dims = values.shape
    spot = [jax.random.randint(jax.random.fold_in(stream_key, axis), (), 0, dims[axis]) for axis in range(len(dims))]
    values = values.at[tuple(spot)].set(least)
    longest = dims.index(max(dims))
    spot[longest] = (spot[longest] + 1) % dims[longest]
    return values.at[tuple(spot)].set(high)


def shard_levels(own_key, dims, shards, least, largest):
    def one(axis_at, blocks):
        heights = jax.random.uniform(jax.random.fold_in(jax.random.fold_in(own_key, 6), axis_at), (blocks,), jnp.float32, least / len(shards), largest / len(shards))
        return jnp.repeat(jnp.exp(heights), dims[axis_at] // blocks).reshape((-1,) + (1,) * (len(dims) - axis_at - 1))

    factor_of = one(*shards[0])
    for cut in shards[1:]:
        factor_of = factor_of * one(*cut)
    return factor_of


def bell_draw(key, extent, spread, bound, shards=(), kind=jnp.bfloat16):
    entries = jax.random.normal(key, extent, jnp.float32) * spread
    if len(shards) > 0:
        entries = shard_levels(key, extent, shards, -0.22, 0.18) * entries
    return jnp.clip(entries, min=-bound, max=bound).astype(kind)


def setup_inputs(seed: int = 0) -> dict:
    keys = jax.random.split(jax.random.key(seed), 12)
    return {
        "efield": bell_draw(keys[0], (3, NX, NY, NZ), 1.0, 6.0, ((1, 8), (2, 4)), jnp.float32),
        "hfield": bell_draw(keys[1], (3, NX, NY, NZ), 1.0, 6.0, ((1, 8), (2, 4)), jnp.float32),
        "polar": bell_draw(keys[2], (3, NX, NY, NZ), 1.0, 6.0, ((1, 8), (2, 4)), jnp.float32),
        "material_map": touch_ends(jax.random.randint(keys[3], (NX, NY, NZ), 0, 3), jax.random.fold_in(keys[3], 1), 0, 2).astype(jnp.int32),
        "via_index": touch_ends(jax.random.randint(keys[4], (NX, NY, NZ), 0, VIAS), jax.random.fold_in(keys[4], 1), 0, VIAS - 1).astype(jnp.int32),
        "fill_fraction": jnp.clip(1.0 * jax.random.uniform(keys[5], (NX, NY, NZ), jnp.float32) ** shard_levels(keys[5], (NX, NY, NZ), ((0, 8), (1, 4)), -0.2, 0.2), 0.0, 1.0),
        "permittivity": jnp.clip(jnp.exp(jax.random.uniform(keys[6], (NMAT,), jnp.float32, math.log(1.0), math.log(5.0))), 1.0, 5.0),
        "conductivity": jnp.clip(jax.random.uniform(keys[7], (NMAT,), jnp.float32, 0.0, 2.0), 0.0, 2.0),
        "debye_strength": jnp.clip(jax.random.uniform(keys[8], (NMAT,), jnp.float32, 0.5, 3.0), 0.5, 3.0),
        "relax_time": jnp.clip(jnp.exp(jax.random.uniform(keys[9], (NMAT,), jnp.float32, math.log(0.5), math.log(5.0))), 0.5, 5.0),
        "conformal": jnp.clip(jax.random.uniform(keys[10], (VIAS, 3), jnp.float32, 0.3, 1.0), 0.3, 1.0),
    }


time_step = 0.55


def select(ids, table, count):
    total = jnp.zeros(ids.shape, jnp.float32)
    for entry in range(count):
        total = total + jnp.where(ids == entry, table[entry], jnp.zeros((), table.dtype))
    return total


def coefficients(material_map, via_index, fill_fraction, permittivity, conductivity, debye_strength, relax_time, conformal):
    count = permittivity.shape[0]
    eps = select(material_map, permittivity, count) * (1.0 + fill_fraction)
    loss = select(material_map, conductivity, count) * time_step / (2.0 * eps)
    ca_coef = (1.0 - loss) / (1.0 + loss)
    cb_coef = time_step / (eps * (1.0 + loss))
    cbp_coef = cb_coef / time_step
    relax = select(material_map, relax_time, count)
    kp_coef = (2.0 * relax - time_step) / (2.0 * relax + time_step)
    bp_coef = 2.0 * time_step * select(material_map, debye_strength, count) / (2.0 * relax + time_step)
    vias = conformal.shape[0]
    weights = [cb_coef * select(via_index, conformal[:, comp], vias) for comp in range(3)]
    return jnp.stack([ca_coef, cbp_coef, kp_coef, bp_coef] + weights)


def forward(field, axis, plane):
    rest = lax.slice_in_dim(field, 1, field.shape[axis], axis=axis)
    return jnp.concatenate([rest, plane], axis=axis)


def backward(field, axis, plane):
    rest = lax.slice_in_dim(field, 0, field.shape[axis] - 1, axis=axis)
    return jnp.concatenate([plane, rest], axis=axis)


def curl_e(efield, y_next, x_next):
    ex_comp, ey_comp, ez_comp = efield[0], efield[1], efield[2]
    z_plane = jnp.zeros_like(ex_comp[:, :, :1])
    cx_part = (forward(ez_comp, 1, y_next[1]) - ez_comp) - (forward(ey_comp, 2, z_plane) - ey_comp)
    cy_part = (forward(ex_comp, 2, z_plane) - ex_comp) - (forward(ez_comp, 0, x_next[1]) - ez_comp)
    cz_part = (forward(ey_comp, 0, x_next[0]) - ey_comp) - (forward(ex_comp, 1, y_next[0]) - ex_comp)
    return jnp.stack([cx_part, cy_part, cz_part])


def curl_h(hfield, y_prev, x_prev):
    hx_comp, hy_comp, hz_comp = hfield[0], hfield[1], hfield[2]
    z_plane = jnp.zeros_like(hx_comp[:, :, :1])
    cx_part = (hz_comp - backward(hz_comp, 1, y_prev[1])) - (hy_comp - backward(hy_comp, 2, z_plane))
    cy_part = (hx_comp - backward(hx_comp, 2, z_plane)) - (hz_comp - backward(hz_comp, 0, x_prev[1]))
    cz_part = (hy_comp - backward(hy_comp, 0, x_prev[0])) - (hx_comp - backward(hx_comp, 1, y_prev[0]))
    return jnp.stack([cx_part, cy_part, cz_part])


def reference(efield, hfield, polar, material_map, via_index, fill_fraction, permittivity, conductivity, debye_strength, relax_time, conformal):
    coef = coefficients(material_map, via_index, fill_fraction, permittivity, conductivity, debye_strength, relax_time, conformal)
    elec, magn, pol = efield, hfield, polar
    y_zero = jnp.zeros_like(elec[0:2, :, :1])
    x_zero = jnp.zeros_like(elec[0:2, :1])
    for step in range(STEPS):
        magn = magn - time_step * curl_e(elec, y_zero, x_zero)
        pol_new = coef[2] * pol + coef[3] * elec
        elec = coef[0] * elec + coef[4:7] * curl_h(magn, y_zero, x_zero) - coef[1] * (pol_new - pol)
        pol = pol_new
    return elec, magn, pol
```

```python
import functools

import jax
import jax.numpy as jnp
from jax import lax
from jax.experimental import pallas as pl
from jax.experimental.pallas import tpu as pltpu
from jax.sharding import PartitionSpec as P

STEPS = 4
DT = 0.55
PAD = 8
MESH = pl.DeviceIdType.MESH


def z_next(value):
    lanes = value.shape[1]
    lane = lax.broadcasted_iota(jnp.int32, value.shape, 1)
    return jnp.where(lane < lanes - 1, pltpu.roll(value, lanes - 1, 1), 0.0)


def z_prev(value):
    lane = lax.broadcasted_iota(jnp.int32, value.shape, 1)
    return jnp.where(lane > 0, pltpu.roll(value, 1, 1), 0.0)


def row_prev(value):
    row = lax.broadcasted_iota(jnp.int32, value.shape, 0)
    return jnp.where(row > 0, pltpu.roll(value, 1, 0), 0.0)


def at_row(line, row, like):
    rows = lax.broadcasted_iota(jnp.int32, like.shape, 0)
    return jnp.where(rows == row, jnp.broadcast_to(line, like.shape), 0.0)


def kernel(
    sizes,
    perm, cond, deb, relax, conf,
    e_in, h_in, p_in, m_in, v_in, f_in,
    e_out, h_out, p_out,
    E, H, Q, M, V, F, C, W,
    sxe, sxa, sye, sya, sce, sca,
    rxe, rxa, rye, rya, rce, rca,
    in_sem, out_sem, send_sem, recv_sem,
):
    count_x, count_y = sizes
    nx, ny, nz = m_in.shape
    mats, vias = perm.shape[0], conf.shape[0]
    gx, gy = lax.axis_index("gx"), lax.axis_index("gy")
    own = pl.ds(PAD, ny)
    last = nx - 1
    end = PAD + ny - 1

    def loads():
        return [
            pltpu.make_async_copy(e_in, E.at[:, 0:nx, 0:ny], in_sem.at[0]),
            pltpu.make_async_copy(h_in, H.at[:, 1 : nx + 1, PAD : PAD + ny], in_sem.at[1]),
            pltpu.make_async_copy(m_in, M, in_sem.at[2]),
            pltpu.make_async_copy(v_in, V, in_sem.at[3]),
            pltpu.make_async_copy(f_in, F, in_sem.at[4]),
            pltpu.make_async_copy(p_in, Q, in_sem.at[5]),
        ]

    low_x, high_x = gx > 0, gx < count_x - 1
    low_y, high_y = gy > 0, gy < count_y - 1
    routes = [
        ((gx - 1, gy), low_x, sxe, rxe, high_x),
        ((gx + 1, gy), high_x, sxa, rxa, low_x),
        ((gx, gy - 1), low_y, sye, rye, high_y),
        ((gx, gy + 1), high_y, sya, rya, low_y),
        ((gx + 1, gy - 1), high_x & low_y, sce, rce, low_x & high_y),
        ((gx - 1, gy + 1), low_x & high_y, sca, rca, high_x & low_y),
    ]

    barrier = pltpu.get_barrier_semaphore()
    for target, there, _, _, _ in routes:
        @pl.when(there)
        def _(target=target):
            pl.semaphore_signal(barrier, inc=1, device_id=target, device_id_type=MESH)

    for copy in loads():
        copy.start()

    def remote(k, t):
        target, _, source, dest, _ = routes[k]
        return pltpu.make_async_remote_copy(
            src_ref=source.at[t],
            dst_ref=dest.at[t],
            send_sem=send_sem.at[k, t],
            recv_sem=recv_sem.at[k, t],
            device_id=target,
            device_id_type=MESH,
        )

    def send(t):
        for k in range(len(routes)):
            @pl.when(routes[k][1])
            def _(k=k):
                remote(k, t).start()

    def wait_sent(t):
        for k in range(len(routes)):
            @pl.when(routes[k][1])
            def _(k=k):
                remote(k, t).wait_send()

    def wait_arrived(t):
        for k in range(len(routes)):
            @pl.when(routes[k][4])
            def _(k=k):
                remote(k, t).wait_recv()

    for _, _, _, dest, sender in routes:
        @pl.when(jnp.logical_not(sender))
        def _(dest=dest):
            dest[...] = jnp.zeros(dest.shape, jnp.float32)

    for comp in range(3):
        E[comp, nx] = jnp.zeros((ny + PAD, nz), jnp.float32)
        H[comp, 0] = jnp.zeros((ny + PAD, nz), jnp.float32)
        for x in range(nx):
            E[comp, x, ny : ny + PAD] = jnp.zeros((PAD, nz), jnp.float32)
            H[comp, x + 1, 0:PAD] = jnp.zeros((PAD, nz), jnp.float32)

    def stage(t):
        sxe[t] = E[1:3, 0, 0:ny]
        ex = E[0, last, 0:ny]
        sxa[t, 0] = H[1, nx, own] - DT * (z_next(ex) - ex + E[2, last, 0:ny])
        sxa[t, 1] = H[2, nx, own] + DT * (E[1, last, 0:ny] + E[0, last, 1 : ny + 1] - ex)
        sce[t] = E[0, last, 0:8]
        sca[t] = E[1, 0, ny - 8 : ny]
        sye[t, 0] = E[0, 0:nx, 0, :]
        sye[t, 1] = E[2, 0:nx, 0, :]
        ey = E[1, 0:nx, ny - 1, :]
        sya[t, 0] = H[0, 1 : nx + 1, end, :] + DT * (E[2, 0:nx, ny - 1, :] + z_next(ey) - ey)
        sya[t, 1] = H[2, 1 : nx + 1, end, :] - DT * (
            E[1, 1 : nx + 1, ny - 1, :] - ey + E[0, 0:nx, ny - 1, :]
        )

    copies = loads()
    copies[0].wait()
    copies[1].wait()
    stage(0)
    pl.semaphore_wait(barrier, sum(jnp.where(route[1], 1, 0) for route in routes))
    send(0)

    for copy in copies[2:5]:
        copy.wait()
    shape = (ny, nz)
    mat_eps = [jnp.full(shape, perm[m], jnp.float32) for m in range(mats)]
    mat_loss = [jnp.full(shape, cond[m] * (0.5 * DT), jnp.float32) for m in range(mats)]
    mat_kp, mat_bp = [], []
    for m in range(mats):
        tau = jnp.full(shape, 2.0 * relax[m], jnp.float32)
        mat_kp.append((tau - DT) / (tau + DT))
        mat_bp.append(jnp.full(shape, 2.0 * DT * deb[m], jnp.float32) / (tau + DT))

    def pick(ids, table):
        value = table[-1]
        for entry in range(len(table) - 2, -1, -1):
            value = jnp.where(ids == entry, table[entry], value)
        return value

    def coefficients(x, carry):
        ids, rows = M[x], V[x]
        eps = pick(ids, mat_eps) * (1.0 + F[x])
        loss = pick(ids, mat_loss)
        kp, bp = pick(ids, mat_kp), pick(ids, mat_bp)
        inv = 1.0 / (eps + loss)
        C[0, x] = (eps - loss - bp) * inv
        C[1, x] = (1.0 - kp) * inv
        C[2, x] = kp
        C[3, x] = bp
        inv = inv * DT
        for comp in range(3):
            C[4 + comp, x] = inv * pick(rows, [conf[row, comp] for row in range(vias)])
        return carry

    lax.fori_loop(0, nx, coefficients, 0, unroll=2)
    for comp in range(3):
        W[comp, 0] = C[4 + comp, :, 0, :]
        W[comp, 1] = C[4 + comp, :, ny - 1, :]
    copies[5].wait()

    flag_x = jnp.where(low_x, 1.0, 0.0)
    flag_y = jnp.where(low_y, 1.0, 0.0)

    def interior(x, carry):
        ex, ey, ez = E[0, x, 0:ny], E[1, x, 0:ny], E[2, x, 0:ny]
        ex_y, ez_y = E[0, x, 1 : ny + 1], E[2, x, 1 : ny + 1]
        ey_x, ez_x = E[1, x + 1, 0:ny], E[2, x + 1, 0:ny]
        hx = H[0, x + 1, own] - DT * ((ez_y - ez) - (z_next(ey) - ey))
        hy = H[1, x + 1, own] - DT * ((z_next(ex) - ex) - (ez_x - ez))
        hz = H[2, x + 1, own] - DT * ((ey_x - ey) - (ex_y - ex))
        H[0, x + 1, own], H[1, x + 1, own], H[2, x + 1, own] = hx, hy, hz
        below = pl.ds(PAD - 1, ny)
        cx = (hz - H[2, x + 1, below]) - (hy - z_prev(hy))
        cy = (hx - z_prev(hx)) - (hz - H[2, x, own])
        cz = (hy - H[1, x, own]) - (hx - H[0, x + 1, below])
        c1, c2, kp, bp = C[0, x], C[1, x], C[2, x], C[3, x]
        for comp, (value, curl) in enumerate(((ex, cx), (ey, cy), (ez, cz))):
            pol = Q[comp, x]
            E[comp, x, 0:ny] = c1 * value + c2 * pol + C[4 + comp, x] * curl
            Q[comp, x] = kp * pol + bp * value
        return carry

    def correct(t):
        dhx, dhz = -DT * rye[t, 1], DT * rye[t, 0]
        H[0, 1 : nx + 1, end, :] += dhx
        H[2, 1 : nx + 1, end, :] += dhz
        E[0, 0:nx, ny - 1, :] += W[0, 1] * dhz
        E[1, 0:nx, ny - 1, :] += W[1, 1] * ((dhx - z_prev(dhx)) - (dhz - row_prev(dhz)))
        E[2, 0:nx, ny - 1, :] -= W[2, 1] * dhx
        hx = flag_y * (rya[t, 0] - DT * sye[t, 1])
        hz = flag_y * (rya[t, 1] + DT * (sye[t, 0] - at_row(rca[t, 7:8], last, dhx)))
        E[0, 0:nx, 0, :] -= W[0, 0] * hz
        E[2, 0:nx, 0, :] += W[2, 0] * hx
        dhy, dhz = DT * rxe[t, 1], -DT * rxe[t, 0]
        H[1, nx, own] += dhy
        H[2, nx, own] += dhz
        E[0, last, 0:ny] += C[4, last] * ((dhz - row_prev(dhz)) - (dhy - z_prev(dhy)))
        E[1, last, 0:ny] -= C[5, last] * dhz
        E[2, last, 0:ny] += C[6, last] * dhy
        hy = flag_x * (rxa[t, 0] + DT * sxe[t, 1])
        hz = flag_x * (rxa[t, 1] - DT * (sxe[t, 0] - at_row(rce[t, 0:1], ny - 1, dhy)))
        E[1, 0, 0:ny] += C[5, 0] * hz
        E[2, 0, 0:ny] -= C[6, 0] * hy

    def advance(t, carry):
        lax.fori_loop(0, nx, interior, 0, unroll=2)
        wait_arrived(t)
        correct(t)

        @pl.when(t < STEPS - 1)
        def _():
            stage(t + 1)
            send(t + 1)

        wait_sent(t)
        return carry

    lax.fori_loop(0, STEPS, advance, 0)

    outs = [
        pltpu.make_async_copy(E.at[:, 0:nx, 0:ny], e_out, out_sem.at[0]),
        pltpu.make_async_copy(H.at[:, 1 : nx + 1, PAD : PAD + ny], h_out, out_sem.at[1]),
        pltpu.make_async_copy(Q, p_out, out_sem.at[2]),
    ]
    for copy in outs:
        copy.start()
    for copy in outs:
        copy.wait()


def shards(sizes, efield, hfield, polar, material_map, via_index, fill, perm, cond, deb, relax, conf):
    nx, ny, nz = material_map.shape
    f32 = jnp.float32
    block = jax.ShapeDtypeStruct(efield.shape, f32)
    planes = [
        pltpu.VMEM((STEPS, 2, ny, nz), f32),
        pltpu.VMEM((STEPS, 2, ny, nz), f32),
        pltpu.VMEM((STEPS, 2, nx, nz), f32),
        pltpu.VMEM((STEPS, 2, nx, nz), f32),
        pltpu.VMEM((STEPS, 8, nz), f32),
        pltpu.VMEM((STEPS, 8, nz), f32),
    ]
    smem = pl.BlockSpec(memory_space=pltpu.SMEM)
    hbm = pl.BlockSpec(memory_space=pl.ANY)
    return pl.pallas_call(
        functools.partial(kernel, sizes),
        out_shape=(block, block, block),
        in_specs=[smem] * 5 + [hbm] * 6,
        out_specs=(hbm, hbm, hbm),
        scratch_shapes=[
            pltpu.VMEM((3, nx + 1, ny + PAD, nz), f32),
            pltpu.VMEM((3, nx + 1, ny + PAD, nz), f32),
            pltpu.VMEM((3, nx, ny, nz), f32),
            pltpu.VMEM((nx, ny, nz), jnp.int32),
            pltpu.VMEM((nx, ny, nz), jnp.int32),
            pltpu.VMEM((nx, ny, nz), f32),
            pltpu.VMEM((7, nx, ny, nz), f32),
            pltpu.VMEM((3, 2, nx, nz), f32),
        ]
        + planes
        + planes
        + [
            pltpu.SemaphoreType.DMA((6,)),
            pltpu.SemaphoreType.DMA((3,)),
            pltpu.SemaphoreType.DMA((6, STEPS)),
            pltpu.SemaphoreType.DMA((6, STEPS)),
        ],
        compiler_params=pltpu.CompilerParams(
            collective_id=0, has_side_effects=True, vmem_limit_bytes=32 * 1024 * 1024
        ),
        cost_estimate=pl.CostEstimate(
            flops=80 * STEPS * nx * ny * nz, bytes_accessed=21 * 4 * nx * ny * nz, transcendentals=0
        ),
        name="yee_steps",
    )(perm, cond, deb, relax, conf, efield, hfield, polar, material_map, via_index, fill)


def solution(mesh):
    field, cell = P(None, "gx", "gy", None), P("gx", "gy", None)
    return jax.shard_map(
        functools.partial(shards, (mesh.shape["gx"], mesh.shape["gy"])),
        mesh=mesh,
        in_specs=(field, field, field, cell, cell, cell, P(), P(), P(), P(), P()),
        out_specs=(field, field, field),
        check_vma=False,
    )
```

```python
import functools

import jax
import jax.numpy as jnp
from jax import lax
from jax.experimental import pallas as pl
from jax.experimental.pallas import tpu as pltpu
from jax.sharding import PartitionSpec as P

STEPS = 4
DT = 0.55
PAD = 8
MESH = pl.DeviceIdType.MESH


def z_next(value):
    lanes = value.shape[1]
    lane = lax.broadcasted_iota(jnp.int32, value.shape, 1)
    return jnp.where(lane < lanes - 1, pltpu.roll(value, lanes - 1, 1), 0.0)


def z_prev(value):
    lane = lax.broadcasted_iota(jnp.int32, value.shape, 1)
    return jnp.where(lane > 0, pltpu.roll(value, 1, 1), 0.0)


def row_prev(value):
    row = lax.broadcasted_iota(jnp.int32, value.shape, 0)
    return jnp.where(row > 0, pltpu.roll(value, 1, 0), 0.0)


def at_row(line, row, like):
    rows = lax.broadcasted_iota(jnp.int32, like.shape, 0)
    return jnp.where(rows == row, jnp.broadcast_to(line, like.shape), 0.0)


def kernel(
    sizes,
    perm, cond, deb, relax, conf,
    e_in, h_in, p_in, m_in, v_in, f_in,
    E, H, Q,
    M, V, F, C, W,
    sxe, sxa, sye, sya, sce, sca,
    rxe, rxa, rye, rya, rce, rca,
    in_sem, send_sem, recv_sem,
):
    count_x, count_y = sizes
    nx, ny, nz = m_in.shape
    mats, vias = perm.shape[0], conf.shape[1]
    gx, gy = lax.axis_index("gx"), lax.axis_index("gy")
    own = pl.ds(PAD, ny)
    last = nx - 1
    end = PAD + ny - 1

    def loads():
        return [
            pltpu.make_async_copy(e_in, E.at[:, 0:nx, 0:ny], in_sem.at[0]),
            pltpu.make_async_copy(h_in, H.at[:, 1 : nx + 1, PAD : PAD + ny], in_sem.at[1]),
            pltpu.make_async_copy(m_in, M, in_sem.at[2]),
            pltpu.make_async_copy(v_in, V, in_sem.at[3]),
            pltpu.make_async_copy(f_in, F, in_sem.at[4]),
            pltpu.make_async_copy(p_in, Q, in_sem.at[5]),
        ]

    low_x, high_x = gx > 0, gx < count_x - 1
    low_y, high_y = gy > 0, gy < count_y - 1
    routes = [
        ((gx - 1, gy), low_x, sxe, rxe, high_x),
        ((gx + 1, gy), high_x, sxa, rxa, low_x),
        ((gx, gy - 1), low_y, sye, rye, high_y),
        ((gx, gy + 1), high_y, sya, rya, low_y),
        ((gx + 1, gy - 1), high_x & low_y, sce, rce, low_x & high_y),
        ((gx - 1, gy + 1), low_x & high_y, sca, rca, high_x & low_y),
    ]

    barrier = pltpu.get_barrier_semaphore()
    for target, there, _, _, _ in routes:
        @pl.when(there)
        def _(target=target):
            pl.semaphore_signal(barrier, inc=1, device_id=target, device_id_type=MESH)

    for copy in loads():
        copy.start()

    def remote(k, t):
        target, _, source, dest, _ = routes[k]
        return pltpu.make_async_remote_copy(
            src_ref=source.at[t],
            dst_ref=dest.at[t],
            send_sem=send_sem.at[k, t],
            recv_sem=recv_sem.at[k, t],
            device_id=target,
            device_id_type=MESH,
        )

    def send(t):
        for k in range(len(routes)):
            @pl.when(routes[k][1])
            def _(k=k):
                remote(k, t).start()

    def wait_sent(t):
        for k in range(len(routes)):
            @pl.when(routes[k][1])
            def _(k=k):
                remote(k, t).wait_send()

    def wait_arrived(t):
        for k in range(len(routes)):
            @pl.when(routes[k][4])
            def _(k=k):
                remote(k, t).wait_recv()

    for _, _, _, dest, sender in routes:
        @pl.when(jnp.logical_not(sender))
        def _(dest=dest):
            dest[...] = jnp.zeros(dest.shape, jnp.float32)

    for comp in range(3):
        E[comp, nx] = jnp.zeros((ny + PAD, nz), jnp.float32)
        H[comp, 0] = jnp.zeros((ny + PAD, nz), jnp.float32)
        for x in range(nx):
            E[comp, x, ny : ny + PAD] = jnp.zeros((PAD, nz), jnp.float32)
            H[comp, x + 1, 0:PAD] = jnp.zeros((PAD, nz), jnp.float32)

    def stage(t):
        sxe[t] = E[1:3, 0, 0:ny]
        ex = E[0, last, 0:ny]
        sxa[t, 0] = H[1, nx, own] - DT * (z_next(ex) - ex + E[2, last, 0:ny])
        sxa[t, 1] = H[2, nx, own] + DT * (E[1, last, 0:ny] + E[0, last, 1 : ny + 1] - ex)
        sce[t] = E[0, last, 0:8]
        sca[t] = E[1, 0, ny - 8 : ny]
        sye[t, 0] = E[0, 0:nx, 0, :]
        sye[t, 1] = E[2, 0:nx, 0, :]
        ey = E[1, 0:nx, ny - 1, :]
        sya[t, 0] = H[0, 1 : nx + 1, end, :] + DT * (E[2, 0:nx, ny - 1, :] + z_next(ey) - ey)
        sya[t, 1] = H[2, 1 : nx + 1, end, :] - DT * (
            E[1, 1 : nx + 1, ny - 1, :] - ey + E[0, 0:nx, ny - 1, :]
        )

    copies = loads()
    copies[0].wait()
    copies[1].wait()
    stage(0)
    pl.semaphore_wait(barrier, sum(jnp.where(route[1], 1, 0) for route in routes))
    send(0)

    for copy in copies[2:5]:
        copy.wait()
    shape = (ny, nz)
    mat_eps = [jnp.full(shape, perm[m], jnp.float32) for m in range(mats)]
    mat_loss = [jnp.full(shape, cond[m] * (0.5 * DT), jnp.float32) for m in range(mats)]
    mat_kp, mat_bp = [], []
    for m in range(mats):
        tau = jnp.full(shape, 2.0 * relax[m], jnp.float32)
        mat_kp.append((tau - DT) / (tau + DT))
        mat_bp.append(jnp.full(shape, 2.0 * DT * deb[m], jnp.float32) / (tau + DT))

    def pick(ids, table):
        value = table[-1]
        for entry in range(len(table) - 2, -1, -1):
            value = jnp.where(ids == entry, table[entry], value)
        return value

    def coefficients(x, carry):
        ids, rows = M[x], V[x]
        eps = pick(ids, mat_eps) * (1.0 + F[x])
        loss = pick(ids, mat_loss)
        kp, bp = pick(ids, mat_kp), pick(ids, mat_bp)
        inv = 1.0 / (eps + loss)
        C[0, x] = (eps - loss - bp) * inv
        C[1, x] = (1.0 - kp) * inv
        C[2, x] = kp
        C[3, x] = bp
        inv = inv * DT
        for comp in range(3):
            C[4 + comp, x] = inv * pick(rows, [conf[comp, row] for row in range(vias)])
        return carry

    lax.fori_loop(0, nx, coefficients, 0, unroll=2)
    for comp in range(3):
        W[comp, 0] = C[4 + comp, :, 0, :]
        W[comp, 1] = C[4 + comp, :, ny - 1, :]
    copies[5].wait()

    flag_x = jnp.where(low_x, 1.0, 0.0)
    flag_y = jnp.where(low_y, 1.0, 0.0)

    def interior(x, carry):
        ex, ey, ez = E[0, x, 0:ny], E[1, x, 0:ny], E[2, x, 0:ny]
        ex_y, ez_y = E[0, x, 1 : ny + 1], E[2, x, 1 : ny + 1]
        ey_x, ez_x = E[1, x + 1, 0:ny], E[2, x + 1, 0:ny]
        hx = H[0, x + 1, own] - DT * ((ez_y - ez) - (z_next(ey) - ey))
        hy = H[1, x + 1, own] - DT * ((z_next(ex) - ex) - (ez_x - ez))
        hz = H[2, x + 1, own] - DT * ((ey_x - ey) - (ex_y - ex))
        H[0, x + 1, own], H[1, x + 1, own], H[2, x + 1, own] = hx, hy, hz
        below = pl.ds(PAD - 1, ny)
        cx = (hz - H[2, x + 1, below]) - (hy - z_prev(hy))
        cy = (hx - z_prev(hx)) - (hz - H[2, x, own])
        cz = (hy - H[1, x, own]) - (hx - H[0, x + 1, below])
        c1, c2, kp, bp = C[0, x], C[1, x], C[2, x], C[3, x]
        for comp, (value, curl) in enumerate(((ex, cx), (ey, cy), (ez, cz))):
            pol = Q[comp, x]
            E[comp, x, 0:ny] = c1 * value + c2 * pol + C[4 + comp, x] * curl
            Q[comp, x] = kp * pol + bp * value
        return carry

    def correct(t):
        dhx, dhz = -DT * rye[t, 1], DT * rye[t, 0]
        H[0, 1 : nx + 1, end, :] += dhx
        H[2, 1 : nx + 1, end, :] += dhz
        E[0, 0:nx, ny - 1, :] += W[0, 1] * dhz
        E[1, 0:nx, ny - 1, :] += W[1, 1] * ((dhx - z_prev(dhx)) - (dhz - row_prev(dhz)))
        E[2, 0:nx, ny - 1, :] -= W[2, 1] * dhx
        hx = flag_y * (rya[t, 0] - DT * sye[t, 1])
        hz = flag_y * (rya[t, 1] + DT * (sye[t, 0] - at_row(rca[t, 7:8], last, dhx)))
        E[0, 0:nx, 0, :] -= W[0, 0] * hz
        E[2, 0:nx, 0, :] += W[2, 0] * hx
        dhy, dhz = DT * rxe[t, 1], -DT * rxe[t, 0]
        H[1, nx, own] += dhy
        H[2, nx, own] += dhz
        E[0, last, 0:ny] += C[4, last] * ((dhz - row_prev(dhz)) - (dhy - z_prev(dhy)))
        E[1, last, 0:ny] -= C[5, last] * dhz
        E[2, last, 0:ny] += C[6, last] * dhy
        hy = flag_x * (rxa[t, 0] + DT * sxe[t, 1])
        hz = flag_x * (rxa[t, 1] - DT * (sxe[t, 0] - at_row(rce[t, 0:1], ny - 1, dhy)))
        E[1, 0, 0:ny] += C[5, 0] * hz
        E[2, 0, 0:ny] -= C[6, 0] * hy

    def advance(t, carry):
        lax.fori_loop(0, nx, interior, 0, unroll=4)
        wait_arrived(t)
        correct(t)

        @pl.when(t < STEPS - 1)
        def _():
            stage(t + 1)
            send(t + 1)

        wait_sent(t)
        return carry

    lax.fori_loop(0, STEPS, advance, 0)


def write_out(sizes, E, H, Q, e_out, h_out, p_out, sem):
    nx, ny = sizes
    outs = [
        pltpu.make_async_copy(E.at[:, 0:nx, 0:ny], e_out, sem.at[0]),
        pltpu.make_async_copy(H.at[:, 1 : nx + 1, PAD : PAD + ny], h_out, sem.at[1]),
        pltpu.make_async_copy(Q, p_out, sem.at[2]),
    ]
    for copy in outs:
        copy.start()
    for copy in outs:
        copy.wait()


def shards(sizes, efield, hfield, polar, material_map, via_index, fill, perm, cond, deb, relax, conf):
    nx, ny, nz = material_map.shape
    f32 = jnp.float32
    block = jax.ShapeDtypeStruct(efield.shape, f32)
    planes = [
        pltpu.VMEM((STEPS, 2, ny, nz), f32),
        pltpu.VMEM((STEPS, 2, ny, nz), f32),
        pltpu.VMEM((STEPS, 2, nx, nz), f32),
        pltpu.VMEM((STEPS, 2, nx, nz), f32),
        pltpu.VMEM((STEPS, 8, nz), f32),
        pltpu.VMEM((STEPS, 8, nz), f32),
    ]
    smem = pl.BlockSpec(memory_space=pltpu.SMEM)
    hbm = pl.BlockSpec(memory_space=pltpu.HBM)
    vmem = pl.BlockSpec(memory_space=pltpu.VMEM)
    padded = pltpu.VMEM((3, nx + 1, ny + PAD, nz), f32)
    state = pl.pallas_call(
        functools.partial(kernel, sizes),
        out_shape=(padded, padded, pltpu.VMEM(efield.shape, f32)),
        in_specs=[smem] * 5 + [hbm] * 6,
        out_specs=(vmem, vmem, vmem),
        scratch_shapes=[
            pltpu.VMEM((nx, ny, nz), jnp.int32),
            pltpu.VMEM((nx, ny, nz), jnp.int32),
            pltpu.VMEM((nx, ny, nz), f32),
            pltpu.VMEM((7, nx, ny, nz), f32),
            pltpu.VMEM((3, 2, nx, nz), f32),
        ]
        + planes
        + planes
        + [
            pltpu.SemaphoreType.DMA((6,)),
            pltpu.SemaphoreType.DMA((6, STEPS)),
            pltpu.SemaphoreType.DMA((6, STEPS)),
        ],
        compiler_params=pltpu.CompilerParams(
            collective_id=0, has_side_effects=True, vmem_limit_bytes=56 * 1024 * 1024
        ),
        cost_estimate=pl.CostEstimate(
            flops=80 * STEPS * nx * ny * nz, bytes_accessed=21 * 4 * nx * ny * nz, transcendentals=0
        ),
        name="yee_steps",
    )(perm, cond, deb, relax, conf.T, efield, hfield, polar, material_map, via_index, fill)
    return pl.pallas_call(
        functools.partial(write_out, (nx, ny)),
        out_shape=(block, block, block),
        in_specs=[pl.BlockSpec(memory_space=pl.ANY)] * 3,
        out_specs=(hbm, hbm, hbm),
        scratch_shapes=[pltpu.SemaphoreType.DMA((3,))],
        name="write_out",
    )(*state)


def solution(mesh):
    field, cell = P(None, "gx", "gy", None), P("gx", "gy", None)
    return jax.shard_map(
        functools.partial(shards, (mesh.shape["gx"], mesh.shape["gy"])),
        mesh=mesh,
        in_specs=(field, field, field, cell, cell, cell, P(), P(), P(), P(), P()),
        out_specs=(field, field, field),
        check_vma=False,
    )
```

```python
import functools

import jax
import jax.numpy as jnp
from jax import lax
from jax.experimental import pallas as pl
from jax.experimental.pallas import tpu as pltpu
from jax.sharding import PartitionSpec as P

STEPS = 4
DT = 0.55
PAD = 8
MESH = pl.DeviceIdType.MESH


def z_next(value):
    lanes = value.shape[1]
    lane = lax.broadcasted_iota(jnp.int32, value.shape, 1)
    return jnp.where(lane < lanes - 1, pltpu.roll(value, lanes - 1, 1), 0.0)


def z_prev(value):
    lane = lax.broadcasted_iota(jnp.int32, value.shape, 1)
    return jnp.where(lane > 0, pltpu.roll(value, 1, 1), 0.0)


def row_prev(value):
    row = lax.broadcasted_iota(jnp.int32, value.shape, 0)
    return jnp.where(row > 0, pltpu.roll(value, 1, 0), 0.0)


def at_row(line, row, like):
    rows = lax.broadcasted_iota(jnp.int32, like.shape, 0)
    return jnp.where(rows == row, jnp.broadcast_to(line, like.shape), 0.0)


def kernel(
    sizes,
    perm, cond, deb, relax, conf,
    e_in, h_in, p_in, m_in, v_in, f_in,
    E, H, Q,
    M, V, F, C, W,
    sxe, sxa, sye, sya, sce, sca,
    rxe, rxa, rye, rya, rce, rca,
    in_sem, send_sem, recv_sem,
):
    count_x, count_y = sizes
    nx, ny, nz = m_in.shape
    mats, vias = perm.shape[0], conf.shape[1]
    gx, gy = lax.axis_index("gx"), lax.axis_index("gy")
    own = pl.ds(PAD, ny)
    last = nx - 1
    end = PAD + ny - 1

    height = ny + PAD
    flat_e = E.reshape(3 * (nx + 1) * height, nz)
    flat_h = H.reshape(3 * (nx + 1) * height, nz)

    def line(comp, x, row):
        return pl.ds((comp * (nx + 1) + x) * height + row, nx, stride=height)

    def loads():
        return [
            pltpu.make_async_copy(e_in, E.at[:, 0:nx, 0:ny], in_sem.at[0]),
            pltpu.make_async_copy(h_in, H.at[:, 1 : nx + 1, PAD : PAD + ny], in_sem.at[1]),
            pltpu.make_async_copy(m_in, M, in_sem.at[2]),
            pltpu.make_async_copy(v_in, V, in_sem.at[3]),
            pltpu.make_async_copy(f_in, F, in_sem.at[4]),
            pltpu.make_async_copy(p_in, Q, in_sem.at[5]),
        ]

    low_x, high_x = gx > 0, gx < count_x - 1
    low_y, high_y = gy > 0, gy < count_y - 1
    routes = [
        ((gx - 1, gy), low_x, sxe, rxe, high_x),
        ((gx + 1, gy), high_x, sxa, rxa, low_x),
        ((gx, gy - 1), low_y, sye, rye, high_y),
        ((gx, gy + 1), high_y, sya, rya, low_y),
        ((gx + 1, gy - 1), high_x & low_y, sce, rce, low_x & high_y),
        ((gx - 1, gy + 1), low_x & high_y, sca, rca, high_x & low_y),
    ]

    barrier = pltpu.get_barrier_semaphore()
    for target, there, _, _, _ in routes:
        @pl.when(there)
        def _(target=target):
            pl.semaphore_signal(barrier, inc=1, device_id=target, device_id_type=MESH)

    for copy in loads():
        copy.start()

    def remote(k, t):
        target, _, source, dest, _ = routes[k]
        return pltpu.make_async_remote_copy(
            src_ref=source.at[t],
            dst_ref=dest.at[t],
            send_sem=send_sem.at[k, t],
            recv_sem=recv_sem.at[k, t],
            device_id=target,
            device_id_type=MESH,
        )

    def send(t):
        for k in range(len(routes)):
            @pl.when(routes[k][1])
            def _(k=k):
                remote(k, t).start()

    def wait_sent(t):
        for k in range(len(routes)):
            @pl.when(routes[k][1])
            def _(k=k):
                remote(k, t).wait_send()

    def wait_arrived(t):
        for k in range(len(routes)):
            @pl.when(routes[k][4])
            def _(k=k):
                remote(k, t).wait_recv()

    for _, _, _, dest, sender in routes:
        @pl.when(jnp.logical_not(sender))
        def _(dest=dest):
            dest[...] = jnp.zeros(dest.shape, jnp.float32)

    for comp in range(3):
        E[comp, nx] = jnp.zeros((ny + PAD, nz), jnp.float32)
        H[comp, 0] = jnp.zeros((ny + PAD, nz), jnp.float32)
        for x in range(nx):
            E[comp, x, ny : ny + PAD] = jnp.zeros((PAD, nz), jnp.float32)
            H[comp, x + 1, 0:PAD] = jnp.zeros((PAD, nz), jnp.float32)

    def stage(t):
        sxe[t] = E[1:3, 0, 0:ny]
        ex = E[0, last, 0:ny]
        sxa[t, 0] = H[1, nx, own] - DT * (z_next(ex) - ex + E[2, last, 0:ny])
        sxa[t, 1] = H[2, nx, own] + DT * (E[1, last, 0:ny] + E[0, last, 1 : ny + 1] - ex)
        sce[t] = E[0, last, 0:8]
        sca[t] = E[1, 0, ny - 8 : ny]
        sye[t, 0] = flat_e[line(0, 0, 0), :]
        sye[t, 1] = flat_e[line(2, 0, 0), :]
        ey = flat_e[line(1, 0, ny - 1), :]
        sya[t, 0] = flat_h[line(0, 1, end), :] + DT * (flat_e[line(2, 0, ny - 1), :] + z_next(ey) - ey)
        sya[t, 1] = flat_h[line(2, 1, end), :] - DT * (
            flat_e[line(1, 1, ny - 1), :] - ey + flat_e[line(0, 0, ny - 1), :]
        )

    copies = loads()
    copies[0].wait()
    copies[1].wait()
    stage(0)
    pl.semaphore_wait(barrier, sum(jnp.where(route[1], 1, 0) for route in routes))
    send(0)

    for copy in copies[2:5]:
        copy.wait()
    shape = (ny, nz)
    mat_eps = [jnp.full(shape, perm[m], jnp.float32) for m in range(mats)]
    mat_loss = [jnp.full(shape, cond[m] * (0.5 * DT), jnp.float32) for m in range(mats)]
    mat_kp, mat_bp = [], []
    for m in range(mats):
        tau = jnp.full(shape, 2.0 * relax[m], jnp.float32)
        mat_kp.append((tau - DT) / (tau + DT))
        mat_bp.append(jnp.full(shape, 2.0 * DT * deb[m], jnp.float32) / (tau + DT))

    def pick(ids, table):
        value = table[-1]
        for entry in range(len(table) - 2, -1, -1):
            value = jnp.where(ids == entry, table[entry], value)
        return value

    def coefficients(x, carry):
        ids, rows = M[x], V[x]
        eps = pick(ids, mat_eps) * (1.0 + F[x])
        loss = pick(ids, mat_loss)
        kp, bp = pick(ids, mat_kp), pick(ids, mat_bp)
        inv = 1.0 / (eps + loss)
        C[0, x] = (eps - loss - bp) * inv
        C[1, x] = (1.0 - kp) * inv
        C[2, x] = kp
        C[3, x] = bp
        inv = inv * DT
        for comp in range(3):
            C[4 + comp, x] = inv * pick(rows, [conf[comp, row] for row in range(vias)])
        return carry

    lax.fori_loop(0, nx, coefficients, 0, unroll=4)
    for comp in range(3):
        W[comp, 0] = C[4 + comp, :, 0, :]
        W[comp, 1] = C[4 + comp, :, ny - 1, :]
    copies[5].wait()

    flag_x = jnp.where(low_x, 1.0, 0.0)
    flag_y = jnp.where(low_y, 1.0, 0.0)

    def update_h(x, carry):
        ex, ey, ez = E[0, x, 0:ny], E[1, x, 0:ny], E[2, x, 0:ny]
        ex_y, ez_y = E[0, x, 1 : ny + 1], E[2, x, 1 : ny + 1]
        ey_x, ez_x = E[1, x + 1, 0:ny], E[2, x + 1, 0:ny]
        H[0, x + 1, own] = H[0, x + 1, own] - DT * ((ez_y - ez) - (z_next(ey) - ey))
        H[1, x + 1, own] = H[1, x + 1, own] - DT * ((z_next(ex) - ex) - (ez_x - ez))
        H[2, x + 1, own] = H[2, x + 1, own] - DT * ((ey_x - ey) - (ex_y - ex))
        return carry

    def update_e(x, carry):
        hx, hy, hz = H[0, x + 1, own], H[1, x + 1, own], H[2, x + 1, own]
        below = pl.ds(PAD - 1, ny)
        cx = (hz - H[2, x + 1, below]) - (hy - z_prev(hy))
        cy = (hx - z_prev(hx)) - (hz - H[2, x, own])
        cz = (hy - H[1, x, own]) - (hx - H[0, x + 1, below])
        c1, c2, kp, bp = C[0, x], C[1, x], C[2, x], C[3, x]
        for comp, curl in enumerate((cx, cy, cz)):
            value, pol = E[comp, x, 0:ny], Q[comp, x]
            E[comp, x, 0:ny] = c1 * value + c2 * pol + C[4 + comp, x] * curl
            Q[comp, x] = kp * pol + bp * value
        return carry

    def correct(t):
        dhx, dhz = -DT * rye[t, 1], DT * rye[t, 0]
        flat_h[line(0, 1, end), :] += dhx
        flat_h[line(2, 1, end), :] += dhz
        flat_e[line(0, 0, ny - 1), :] += W[0, 1] * dhz
        flat_e[line(1, 0, ny - 1), :] += W[1, 1] * ((dhx - z_prev(dhx)) - (dhz - row_prev(dhz)))
        flat_e[line(2, 0, ny - 1), :] -= W[2, 1] * dhx
        hx = flag_y * (rya[t, 0] - DT * sye[t, 1])
        hz = flag_y * (rya[t, 1] + DT * (sye[t, 0] - at_row(rca[t, 7:8], last, dhx)))
        flat_e[line(0, 0, 0), :] -= W[0, 0] * hz
        flat_e[line(2, 0, 0), :] += W[2, 0] * hx
        dhy, dhz = DT * rxe[t, 1], -DT * rxe[t, 0]
        H[1, nx, own] += dhy
        H[2, nx, own] += dhz
        E[0, last, 0:ny] += C[4, last] * ((dhz - row_prev(dhz)) - (dhy - z_prev(dhy)))
        E[1, last, 0:ny] -= C[5, last] * dhz
        E[2, last, 0:ny] += C[6, last] * dhy
        hy = flag_x * (rxa[t, 0] + DT * sxe[t, 1])
        hz = flag_x * (rxa[t, 1] - DT * (sxe[t, 0] - at_row(rce[t, 0:1], ny - 1, dhy)))
        E[1, 0, 0:ny] += C[5, 0] * hz
        E[2, 0, 0:ny] -= C[6, 0] * hy

    def advance(t, carry):
        lax.fori_loop(0, nx, update_h, 0, unroll=nx)
        lax.fori_loop(0, nx, update_e, 0, unroll=nx)
        wait_arrived(t)
        correct(t)

        @pl.when(t < STEPS - 1)
        def _():
            stage(t + 1)
            send(t + 1)

        wait_sent(t)
        return carry

    lax.fori_loop(0, STEPS, advance, 0)


def write_out(sizes, E, H, Q, e_out, h_out, p_out, sem):
    nx, ny = sizes
    outs = [
        pltpu.make_async_copy(E.at[:, 0:nx, 0:ny], e_out, sem.at[0]),
        pltpu.make_async_copy(H.at[:, 1 : nx + 1, PAD : PAD + ny], h_out, sem.at[1]),
        pltpu.make_async_copy(Q, p_out, sem.at[2]),
    ]
    for copy in outs:
        copy.start()
    for copy in outs:
        copy.wait()


def shards(sizes, efield, hfield, polar, material_map, via_index, fill, perm, cond, deb, relax, conf):
    nx, ny, nz = material_map.shape
    f32 = jnp.float32
    block = jax.ShapeDtypeStruct(efield.shape, f32)
    planes = [
        pltpu.VMEM((STEPS, 2, ny, nz), f32),
        pltpu.VMEM((STEPS, 2, ny, nz), f32),
        pltpu.VMEM((STEPS, 2, nx, nz), f32),
        pltpu.VMEM((STEPS, 2, nx, nz), f32),
        pltpu.VMEM((STEPS, 8, nz), f32),
        pltpu.VMEM((STEPS, 8, nz), f32),
    ]
    smem = pl.BlockSpec(memory_space=pltpu.SMEM)
    hbm = pl.BlockSpec(memory_space=pltpu.HBM)
    vmem = pl.BlockSpec(memory_space=pltpu.VMEM)
    padded = pltpu.VMEM((3, nx + 1, ny + PAD, nz), f32)
    state = pl.pallas_call(
        functools.partial(kernel, sizes),
        out_shape=(padded, padded, pltpu.VMEM(efield.shape, f32)),
        in_specs=[smem] * 5 + [hbm] * 6,
        out_specs=(vmem, vmem, vmem),
        scratch_shapes=[
            pltpu.VMEM((nx, ny, nz), jnp.int32),
            pltpu.VMEM((nx, ny, nz), jnp.int32),
            pltpu.VMEM((nx, ny, nz), f32),
            pltpu.VMEM((7, nx, ny, nz), f32),
            pltpu.VMEM((3, 2, nx, nz), f32),
        ]
        + planes
        + planes
        + [
            pltpu.SemaphoreType.DMA((6,)),
            pltpu.SemaphoreType.DMA((6, STEPS)),
            pltpu.SemaphoreType.DMA((6, STEPS)),
        ],
        compiler_params=pltpu.CompilerParams(
            collective_id=0, has_side_effects=True, vmem_limit_bytes=56 * 1024 * 1024
        ),
        cost_estimate=pl.CostEstimate(
            flops=80 * STEPS * nx * ny * nz, bytes_accessed=21 * 4 * nx * ny * nz, transcendentals=0
        ),
        name="yee_steps",
    )(perm, cond, deb, relax, conf.T, efield, hfield, polar, material_map, via_index, fill)
    return pl.pallas_call(
        functools.partial(write_out, (nx, ny)),
        out_shape=(block, block, block),
        in_specs=[pl.BlockSpec(memory_space=pl.ANY)] * 3,
        out_specs=(hbm, hbm, hbm),
        scratch_shapes=[pltpu.SemaphoreType.DMA((3,))],
        compiler_params=pltpu.CompilerParams(vmem_limit_bytes=4 * 1024 * 1024),
        name="write_out",
    )(*state)


def solution(mesh):
    field, cell = P(None, "gx", "gy", None), P("gx", "gy", None)
    return jax.shard_map(
        functools.partial(shards, (mesh.shape["gx"], mesh.shape["gy"])),
        mesh=mesh,
        in_specs=(field, field, field, cell, cell, cell, P(), P(), P(), P(), P()),
        out_specs=(field, field, field),
        check_vma=False,
    )
```

```python
import functools

import jax
import jax.numpy as jnp
from jax import lax
from jax.experimental import pallas as pl
from jax.experimental.pallas import tpu as pltpu
from jax.sharding import PartitionSpec as P

STEPS = 4
DT = 0.55
PAD = 8
MESH = pl.DeviceIdType.MESH


def z_next(value):
    lanes = value.shape[1]
    lane = lax.broadcasted_iota(jnp.int32, value.shape, 1)
    return jnp.where(lane < lanes - 1, pltpu.roll(value, lanes - 1, 1), 0.0)


def z_prev(value):
    lane = lax.broadcasted_iota(jnp.int32, value.shape, 1)
    return jnp.where(lane > 0, pltpu.roll(value, 1, 1), 0.0)


def row_prev(value):
    row = lax.broadcasted_iota(jnp.int32, value.shape, 0)
    return jnp.where(row > 0, pltpu.roll(value, 1, 0), 0.0)


def at_row(line, row, like):
    rows = lax.broadcasted_iota(jnp.int32, like.shape, 0)
    return jnp.where(rows == row, jnp.broadcast_to(line, like.shape), 0.0)


def kernel(
    sizes,
    perm_in, cond_in, deb_in, relax_in, conf_in,
    e_in, h_in, p_in, m_in, v_in, f_in,
    E, H, Q,
    M, V, F, C, W,
    perm, cond, deb, relax, conf,
    sxe, sxa, sye, sya, sce, sca,
    rxe, rxa, rye, rya, rce, rca,
    in_sem, send_sem, recv_sem,
):
    count_x, count_y = sizes
    nx, ny, nz = m_in.shape
    mats, vias = perm.shape[0], conf.shape[1]
    gx, gy = lax.axis_index("gx"), lax.axis_index("gy")
    own = pl.ds(PAD, ny)
    last = nx - 1
    end = PAD + ny - 1

    height = ny + PAD
    flat_e = E.reshape(3 * (nx + 1) * height, nz)
    flat_h = H.reshape(3 * (nx + 1) * height, nz)

    def line(comp, x, row):
        return pl.ds((comp * (nx + 1) + x) * height + row, nx, stride=height)

    def loads():
        return [
            pltpu.make_async_copy(e_in, E.at[:, 0:nx, 0:ny], in_sem.at[0]),
            pltpu.make_async_copy(h_in, H.at[:, 1 : nx + 1, PAD : PAD + ny], in_sem.at[1]),
            pltpu.make_async_copy(m_in, M, in_sem.at[2]),
            pltpu.make_async_copy(v_in, V, in_sem.at[3]),
            pltpu.make_async_copy(f_in, F, in_sem.at[4]),
            pltpu.make_async_copy(p_in, Q, in_sem.at[5]),
            pltpu.make_async_copy(perm_in, perm, in_sem.at[6]),
            pltpu.make_async_copy(cond_in, cond, in_sem.at[7]),
            pltpu.make_async_copy(deb_in, deb, in_sem.at[8]),
            pltpu.make_async_copy(relax_in, relax, in_sem.at[9]),
            pltpu.make_async_copy(conf_in, conf, in_sem.at[10]),
        ]

    low_x, high_x = gx > 0, gx < count_x - 1
    low_y, high_y = gy > 0, gy < count_y - 1
    routes = [
        ((gx - 1, gy), low_x, sxe, rxe, high_x),
        ((gx + 1, gy), high_x, sxa, rxa, low_x),
        ((gx, gy - 1), low_y, sye, rye, high_y),
        ((gx, gy + 1), high_y, sya, rya, low_y),
        ((gx + 1, gy - 1), high_x & low_y, sce, rce, low_x & high_y),
        ((gx - 1, gy + 1), low_x & high_y, sca, rca, high_x & low_y),
    ]

    barrier = pltpu.get_barrier_semaphore()
    for target, there, _, _, _ in routes:
        @pl.when(there)
        def _(target=target):
            pl.semaphore_signal(barrier, inc=1, device_id=target, device_id_type=MESH)

    for copy in loads():
        copy.start()

    def remote(k, t):
        target, _, source, dest, _ = routes[k]
        return pltpu.make_async_remote_copy(
            src_ref=source.at[t],
            dst_ref=dest.at[t],
            send_sem=send_sem.at[k, t],
            recv_sem=recv_sem.at[k, t],
            device_id=target,
            device_id_type=MESH,
        )

    def each(chosen, which, act):
        for k in chosen:
            @pl.when(routes[k][which])
            def _(k=k):
                act(k)

    def send(t, chosen):
        each(chosen, 1, lambda k: remote(k, t).start())

    def wait_sent(t):
        each(range(6), 1, lambda k: remote(k, t).wait_send())

    def wait_arrived(t, chosen):
        each(chosen, 4, lambda k: remote(k, t).wait_recv())

    for _, _, _, dest, sender in routes:
        @pl.when(jnp.logical_not(sender))
        def _(dest=dest):
            dest[...] = jnp.zeros(dest.shape, jnp.float32)

    for comp in range(3):
        E[comp, nx] = jnp.zeros((ny + PAD, nz), jnp.float32)
        H[comp, 0] = jnp.zeros((ny + PAD, nz), jnp.float32)
        for x in range(nx):
            E[comp, x, ny : ny + PAD] = jnp.zeros((PAD, nz), jnp.float32)
            H[comp, x + 1, 0:PAD] = jnp.zeros((PAD, nz), jnp.float32)

    def stage_x(t):
        sce[t] = E[0, last, 0:8]
        sca[t] = E[1, 0, ny - 8 : ny]
        sxe[t] = E[1:3, 0, 0:ny]
        ex = E[0, last, 0:ny]
        sxa[t, 0] = H[1, nx, own] - DT * (z_next(ex) - ex + E[2, last, 0:ny])
        sxa[t, 1] = H[2, nx, own] + DT * (E[1, last, 0:ny] + E[0, last, 1 : ny + 1] - ex)

    def stage_y(t):
        sye[t, 0] = flat_e[line(0, 0, 0), :]
        sye[t, 1] = flat_e[line(2, 0, 0), :]
        ey = flat_e[line(1, 0, ny - 1), :]
        sya[t, 0] = flat_h[line(0, 1, end), :] + DT * (flat_e[line(2, 0, ny - 1), :] + z_next(ey) - ey)
        sya[t, 1] = flat_h[line(2, 1, end), :] - DT * (
            flat_e[line(1, 1, ny - 1), :] - ey + flat_e[line(0, 0, ny - 1), :]
        )

    def stage_and_send(t):
        stage_x(t)
        send(t, (4, 5, 0, 1))
        stage_y(t)
        send(t, (2, 3))

    copies = loads()
    copies[0].wait()
    copies[1].wait()
    pl.semaphore_wait(barrier, sum(jnp.where(route[1], 1, 0) for route in routes))
    stage_and_send(0)

    for copy in copies[2:5] + copies[6:]:
        copy.wait()
    shape = (ny, nz)
    mat_eps = [jnp.full(shape, perm[m], jnp.float32) for m in range(mats)]
    mat_loss = [jnp.full(shape, cond[m] * (0.5 * DT), jnp.float32) for m in range(mats)]
    mat_kp, mat_bp = [], []
    for m in range(mats):
        tau = jnp.full(shape, 2.0 * relax[m], jnp.float32)
        mat_kp.append((tau - DT) / (tau + DT))
        mat_bp.append(jnp.full(shape, 2.0 * DT * deb[m], jnp.float32) / (tau + DT))

    def pick(ids, table):
        value = table[-1]
        for entry in range(len(table) - 2, -1, -1):
            value = jnp.where(ids == entry, table[entry], value)
        return value

    def coefficients(x, carry):
        ids, rows = M[x], V[x]
        eps = pick(ids, mat_eps) * (1.0 + F[x])
        loss = pick(ids, mat_loss)
        kp, bp = pick(ids, mat_kp), pick(ids, mat_bp)
        inv = 1.0 / (eps + loss)
        C[0, x] = (eps - loss - bp) * inv
        C[1, x] = (1.0 - kp) * inv
        C[2, x] = kp
        C[3, x] = bp
        inv = inv * DT
        for comp in range(3):
            C[4 + comp, x] = inv * pick(rows, [conf[comp, row] for row in range(vias)])
        return carry

    lax.fori_loop(0, nx, coefficients, 0, unroll=4)
    for comp in range(3):
        W[comp, 0] = C[4 + comp, :, 0, :]
        W[comp, 1] = C[4 + comp, :, ny - 1, :]
    copies[5].wait()

    flag_x = jnp.where(low_x, 1.0, 0.0)
    flag_y = jnp.where(low_y, 1.0, 0.0)

    def update_h(x, carry):
        ex, ey, ez = E[0, x, 0:ny], E[1, x, 0:ny], E[2, x, 0:ny]
        ex_y, ez_y = E[0, x, 1 : ny + 1], E[2, x, 1 : ny + 1]
        ey_x, ez_x = E[1, x + 1, 0:ny], E[2, x + 1, 0:ny]
        H[0, x + 1, own] = H[0, x + 1, own] - DT * ((ez_y - ez) - (z_next(ey) - ey))
        H[1, x + 1, own] = H[1, x + 1, own] - DT * ((z_next(ex) - ex) - (ez_x - ez))
        H[2, x + 1, own] = H[2, x + 1, own] - DT * ((ey_x - ey) - (ex_y - ex))
        return carry

    def update_e(x, carry):
        hx, hy, hz = H[0, x + 1, own], H[1, x + 1, own], H[2, x + 1, own]
        below = pl.ds(PAD - 1, ny)
        cx = (hz - H[2, x + 1, below]) - (hy - z_prev(hy))
        cy = (hx - z_prev(hx)) - (hz - H[2, x, own])
        cz = (hy - H[1, x, own]) - (hx - H[0, x + 1, below])
        c1, c2, kp, bp = C[0, x], C[1, x], C[2, x], C[3, x]
        for comp, curl in enumerate((cx, cy, cz)):
            value, pol = E[comp, x, 0:ny], Q[comp, x]
            E[comp, x, 0:ny] = c1 * value + c2 * pol + C[4 + comp, x] * curl
            Q[comp, x] = kp * pol + bp * value
        return carry

    def correct_y(t):
        dhx, dhz = -DT * rye[t, 1], DT * rye[t, 0]
        flat_h[line(0, 1, end), :] += dhx
        flat_h[line(2, 1, end), :] += dhz
        flat_e[line(0, 0, ny - 1), :] += W[0, 1] * dhz
        flat_e[line(1, 0, ny - 1), :] += W[1, 1] * ((dhx - z_prev(dhx)) - (dhz - row_prev(dhz)))
        flat_e[line(2, 0, ny - 1), :] -= W[2, 1] * dhx
        hx = flag_y * (rya[t, 0] - DT * sye[t, 1])
        hz = flag_y * (rya[t, 1] + DT * sye[t, 0])
        flat_e[line(0, 0, 0), :] -= W[0, 0] * hz
        flat_e[line(2, 0, 0), :] += W[2, 0] * hx

    def correct_x(t):
        dhy, dhz = DT * rxe[t, 1], -DT * rxe[t, 0]
        corner = at_row(DT * rca[t, 7:8], 0, dhy)
        E[0, last, 0:ny] += C[4, last] * (
            (dhz - row_prev(dhz)) - (dhy - z_prev(dhy)) + corner
        )
        E[1, last, 0:ny] -= C[5, last] * dhz
        E[2, last, 0:ny] += C[6, last] * dhy
        hy = flag_x * (rxa[t, 0] + DT * sxe[t, 1])
        hz = flag_x * (rxa[t, 1] - DT * (sxe[t, 0] - at_row(rce[t, 0:1], ny - 1, dhy)))
        E[1, 0, 0:ny] += C[5, 0] * hz
        E[2, 0, 0:ny] -= C[6, 0] * hy
        H[1, nx, own] += dhy
        H[2, nx, own] += dhz

    def advance(t, carry):
        lax.fori_loop(0, nx, update_h, 0, unroll=nx)
        lax.fori_loop(0, nx, update_e, 0, unroll=nx)
        wait_arrived(t, (2, 3))
        correct_y(t)
        wait_arrived(t, (4, 5, 0, 1))
        correct_x(t)

        @pl.when(t < STEPS - 1)
        def _():
            stage_and_send(t + 1)

        wait_sent(t)
        return carry

    lax.fori_loop(0, STEPS, advance, 0)


def write_out(sizes, E, H, Q, e_out, h_out, p_out, sem):
    nx, ny = sizes
    outs = [
        pltpu.make_async_copy(E.at[:, 0:nx, 0:ny], e_out, sem.at[0]),
        pltpu.make_async_copy(H.at[:, 1 : nx + 1, PAD : PAD + ny], h_out, sem.at[1]),
        pltpu.make_async_copy(Q, p_out, sem.at[2]),
    ]
    for copy in outs:
        copy.start()
    for copy in outs:
        copy.wait()


def shards(sizes, efield, hfield, polar, material_map, via_index, fill, perm, cond, deb, relax, conf):
    nx, ny, nz = material_map.shape
    f32 = jnp.float32
    block = jax.ShapeDtypeStruct(efield.shape, f32)
    planes = [
        pltpu.VMEM((STEPS, 2, ny, nz), f32),
        pltpu.VMEM((STEPS, 2, ny, nz), f32),
        pltpu.VMEM((STEPS, 2, nx, nz), f32),
        pltpu.VMEM((STEPS, 2, nx, nz), f32),
        pltpu.VMEM((STEPS, 8, nz), f32),
        pltpu.VMEM((STEPS, 8, nz), f32),
    ]
    hbm = pl.BlockSpec(memory_space=pltpu.HBM)
    vmem = pl.BlockSpec(memory_space=pltpu.VMEM)
    padded = pltpu.VMEM((3, nx + 1, ny + PAD, nz), f32)
    state = pl.pallas_call(
        functools.partial(kernel, sizes),
        out_shape=(padded, padded, pltpu.VMEM(efield.shape, f32)),
        in_specs=[hbm] * 11,
        out_specs=(vmem, vmem, vmem),
        scratch_shapes=[
            pltpu.VMEM((nx, ny, nz), jnp.int32),
            pltpu.VMEM((nx, ny, nz), jnp.int32),
            pltpu.VMEM((nx, ny, nz), f32),
            pltpu.VMEM((7, nx, ny, nz), f32),
            pltpu.VMEM((3, 2, nx, nz), f32),
        ]
        + [pltpu.SMEM(table.shape, f32) for table in (perm, cond, deb, relax, conf.T)]
        + planes
        + planes
        + [
            pltpu.SemaphoreType.DMA((11,)),
            pltpu.SemaphoreType.DMA((6, STEPS)),
            pltpu.SemaphoreType.DMA((6, STEPS)),
        ],
        compiler_params=pltpu.CompilerParams(
            collective_id=0, has_side_effects=True, vmem_limit_bytes=56 * 1024 * 1024
        ),
        cost_estimate=pl.CostEstimate(
            flops=80 * STEPS * nx * ny * nz, bytes_accessed=21 * 4 * nx * ny * nz, transcendentals=0
        ),
        name="yee_steps",
    )(perm, cond, deb, relax, conf.T, efield, hfield, polar, material_map, via_index, fill)
    return pl.pallas_call(
        functools.partial(write_out, (nx, ny)),
        out_shape=(block, block, block),
        in_specs=[pl.BlockSpec(memory_space=pl.ANY)] * 3,
        out_specs=(hbm, hbm, hbm),
        scratch_shapes=[pltpu.SemaphoreType.DMA((3,))],
        compiler_params=pltpu.CompilerParams(vmem_limit_bytes=4 * 1024 * 1024),
        name="write_out",
    )(*state)


def solution(mesh):
    field, cell = P(None, "gx", "gy", None), P("gx", "gy", None)
    return jax.shard_map(
        functools.partial(shards, (mesh.shape["gx"], mesh.shape["gy"])),
        mesh=mesh,
        in_specs=(field, field, field, cell, cell, cell, P(), P(), P(), P(), P()),
        out_specs=(field, field, field),
        check_vma=False,
    )
```

```python
import functools

import jax
import jax.numpy as jnp
from jax import lax
from jax.experimental import pallas as pl
from jax.experimental.pallas import tpu as pltpu
from jax.sharding import PartitionSpec as P

STEPS = 4
DT = 0.55
PAD = 8
MESH = pl.DeviceIdType.MESH


def halves(count):
    half = (count + 1) // 2
    return [(0, half), (half, count - half)] if count > 1 else [(0, count)]


def z_next(value):
    lanes = value.shape[1]
    lane = lax.broadcasted_iota(jnp.int32, value.shape, 1)
    return jnp.where(lane < lanes - 1, pltpu.roll(value, lanes - 1, 1), 0.0)


def z_prev(value):
    lane = lax.broadcasted_iota(jnp.int32, value.shape, 1)
    return jnp.where(lane > 0, pltpu.roll(value, 1, 1), 0.0)


def row_prev(value):
    row = lax.broadcasted_iota(jnp.int32, value.shape, 0)
    return jnp.where(row > 0, pltpu.roll(value, 1, 0), 0.0)


def at_row(line, row, like):
    rows = lax.broadcasted_iota(jnp.int32, like.shape, 0)
    return jnp.where(rows == row, jnp.broadcast_to(line, like.shape), 0.0)


def kernel(
    sizes,
    perm_in, cond_in, deb_in, relax_in, conf_in,
    e_in, h_in, p_in, m_in, v_in, f_in,
    E, H, Q,
    M, V, F, C, W,
    perm, cond, deb, relax, conf,
    sxe, sxa, sye, sya, sce, sca,
    rxe, rxa, rye, rya, rce, rca,
    in_sem, send_sem, recv_sem,
):
    count_x, count_y = sizes
    nx, ny, nz = m_in.shape
    mats, vias = perm.shape[0], conf.shape[1]
    gx, gy = lax.axis_index("gx"), lax.axis_index("gy")
    own = pl.ds(PAD, ny)
    last = nx - 1
    end = PAD + ny - 1

    height = ny + PAD
    flat_e = E.reshape(3 * (nx + 1) * height, nz)
    flat_h = H.reshape(3 * (nx + 1) * height, nz)

    def line(comp, x, row):
        return pl.ds((comp * (nx + 1) + x) * height + row, nx, stride=height)

    def loads():
        fields = []
        for comp in range(3):
            for x, wide in halves(nx):
                part = (comp, pl.ds(x, wide))
                fields.append((e_in.at[part], E.at[comp, pl.ds(x, wide), pl.ds(0, ny)]))
                fields.append((h_in.at[part], H.at[comp, pl.ds(x + 1, wide), own]))
        tables = [(perm_in, perm), (cond_in, cond), (deb_in, deb), (relax_in, relax), (conf_in, conf)]
        cells = [(m_in, M), (v_in, V), (f_in, F)]
        pols = [(p_in.at[comp], Q.at[comp]) for comp in range(3)]
        pairs = fields + tables + cells + pols
        copies = [pltpu.make_async_copy(a, b, in_sem.at[k]) for k, (a, b) in enumerate(pairs)]
        cut = len(fields)
        end_cells = cut + len(tables) + len(cells)
        return copies[:cut], copies[cut:end_cells], copies[end_cells:]

    low_x, high_x = gx > 0, gx < count_x - 1
    low_y, high_y = gy > 0, gy < count_y - 1
    routes = [
        ((gx - 1, gy), low_x, sxe, rxe, high_x),
        ((gx + 1, gy), high_x, sxa, rxa, low_x),
        ((gx, gy - 1), low_y, sye, rye, high_y),
        ((gx, gy + 1), high_y, sya, rya, low_y),
        ((gx + 1, gy - 1), high_x & low_y, sce, rce, low_x & high_y),
        ((gx - 1, gy + 1), low_x & high_y, sca, rca, high_x & low_y),
    ]

    barrier = pltpu.get_barrier_semaphore()
    for target, there, _, _, _ in routes:
        @pl.when(there)
        def _(target=target):
            pl.semaphore_signal(barrier, inc=1, device_id=target, device_id_type=MESH)

    first, second, third = loads()
    for copy in first + second + third:
        copy.start()

    def remote(k, t):
        target, _, source, dest, _ = routes[k]
        return pltpu.make_async_remote_copy(
            src_ref=source.at[t],
            dst_ref=dest.at[t],
            send_sem=send_sem.at[k, t],
            recv_sem=recv_sem.at[k, t],
            device_id=target,
            device_id_type=MESH,
        )

    def each(chosen, which, act):
        for k in chosen:
            @pl.when(routes[k][which])
            def _(k=k):
                act(k)

    def send(t, chosen):
        each(chosen, 1, lambda k: remote(k, t).start())

    def wait_sent(t):
        each(range(6), 1, lambda k: remote(k, t).wait_send())

    def wait_arrived(t, chosen):
        each(chosen, 4, lambda k: remote(k, t).wait_recv())

    for _, _, _, dest, sender in routes:
        @pl.when(jnp.logical_not(sender))
        def _(dest=dest):
            dest[...] = jnp.zeros(dest.shape, jnp.float32)

    for comp in range(3):
        E[comp, nx] = jnp.zeros((ny + PAD, nz), jnp.float32)
        H[comp, 0] = jnp.zeros((ny + PAD, nz), jnp.float32)
        for x in range(nx):
            E[comp, x, ny : ny + PAD] = jnp.zeros((PAD, nz), jnp.float32)
            H[comp, x + 1, 0:PAD] = jnp.zeros((PAD, nz), jnp.float32)

    def stage_first(t):
        sca[t] = E[1, 0, ny - 8 : ny]
        sxe[t] = E[1:3, 0, 0:ny]

    def stage_last(t):
        sce[t] = E[0, last, 0:8]
        ex = E[0, last, 0:ny]
        sxa[t, 0] = H[1, nx, own] - DT * (z_next(ex) - ex + E[2, last, 0:ny])
        sxa[t, 1] = H[2, nx, own] + DT * (E[1, last, 0:ny] + E[0, last, 1 : ny + 1] - ex)

    def stage_y(t):
        sye[t, 0] = flat_e[line(0, 0, 0), :]
        sye[t, 1] = flat_e[line(2, 0, 0), :]
        ey = flat_e[line(1, 0, ny - 1), :]
        sya[t, 0] = flat_h[line(0, 1, end), :] + DT * (flat_e[line(2, 0, ny - 1), :] + z_next(ey) - ey)
        sya[t, 1] = flat_h[line(2, 1, end), :] - DT * (
            flat_e[line(1, 1, ny - 1), :] - ey + flat_e[line(0, 0, ny - 1), :]
        )

    for copy in first:
        copy.wait()
    pl.semaphore_wait(barrier, sum(jnp.where(route[1], 1, 0) for route in routes))
    stage_first(0)
    send(0, (5, 0))
    stage_last(0)
    send(0, (4, 1))
    stage_y(0)
    send(0, (2, 3))

    for copy in second:
        copy.wait()
    shape = (ny, nz)
    mat_eps = [jnp.full(shape, perm[m], jnp.float32) for m in range(mats)]
    mat_loss = [jnp.full(shape, cond[m] * (0.5 * DT), jnp.float32) for m in range(mats)]
    mat_kp, mat_bp = [], []
    for m in range(mats):
        tau = jnp.full(shape, 2.0 * relax[m], jnp.float32)
        mat_kp.append((tau - DT) / (tau + DT))
        mat_bp.append(jnp.full(shape, 2.0 * DT * deb[m], jnp.float32) / (tau + DT))

    def pick(ids, table):
        value = table[-1]
        for entry in range(len(table) - 2, -1, -1):
            value = jnp.where(ids == entry, table[entry], value)
        return value

    def coefficients(x, carry):
        ids, rows = M[x], V[x]
        eps = pick(ids, mat_eps) * (1.0 + F[x])
        loss = pick(ids, mat_loss)
        kp, bp = pick(ids, mat_kp), pick(ids, mat_bp)
        inv = 1.0 / (eps + loss)
        C[0, x] = (eps - loss - bp) * inv
        C[1, x] = (1.0 - kp) * inv
        C[2, x] = kp
        C[3, x] = bp
        inv = inv * DT
        for comp in range(3):
            C[4 + comp, x] = inv * pick(rows, [conf[comp, row] for row in range(vias)])
        return carry

    lax.fori_loop(0, nx, coefficients, 0, unroll=4)
    for comp in range(3):
        W[comp, 0] = C[4 + comp, :, 0, :]
        W[comp, 1] = C[4 + comp, :, ny - 1, :]
    for copy in third:
        copy.wait()

    flag_x = jnp.where(low_x, 1.0, 0.0)
    flag_y = jnp.where(low_y, 1.0, 0.0)

    def update_h(x, carry):
        ex, ey, ez = E[0, x, 0:ny], E[1, x, 0:ny], E[2, x, 0:ny]
        ex_y, ez_y = E[0, x, 1 : ny + 1], E[2, x, 1 : ny + 1]
        ey_x, ez_x = E[1, x + 1, 0:ny], E[2, x + 1, 0:ny]
        H[0, x + 1, own] = H[0, x + 1, own] - DT * ((ez_y - ez) - (z_next(ey) - ey))
        H[1, x + 1, own] = H[1, x + 1, own] - DT * ((z_next(ex) - ex) - (ez_x - ez))
        H[2, x + 1, own] = H[2, x + 1, own] - DT * ((ey_x - ey) - (ex_y - ex))
        return carry

    def update_e(x, carry):
        hx, hy, hz = H[0, x + 1, own], H[1, x + 1, own], H[2, x + 1, own]
        below = pl.ds(PAD - 1, ny)
        cx = (hz - H[2, x + 1, below]) - (hy - z_prev(hy))
        cy = (hx - z_prev(hx)) - (hz - H[2, x, own])
        cz = (hy - H[1, x, own]) - (hx - H[0, x + 1, below])
        c1, c2, kp, bp = C[0, x], C[1, x], C[2, x], C[3, x]
        for comp, curl in enumerate((cx, cy, cz)):
            value, pol = E[comp, x, 0:ny], Q[comp, x]
            E[comp, x, 0:ny] = c1 * value + c2 * pol + C[4 + comp, x] * curl
            Q[comp, x] = kp * pol + bp * value
        return carry

    def correct_y(t):
        dhx, dhz = -DT * rye[t, 1], DT * rye[t, 0]
        flat_h[line(0, 1, end), :] += dhx
        flat_h[line(2, 1, end), :] += dhz
        flat_e[line(0, 0, ny - 1), :] += W[0, 1] * dhz
        flat_e[line(1, 0, ny - 1), :] += W[1, 1] * ((dhx - z_prev(dhx)) - (dhz - row_prev(dhz)))
        flat_e[line(2, 0, ny - 1), :] -= W[2, 1] * dhx
        hx = flag_y * (rya[t, 0] - DT * sye[t, 1])
        hz = flag_y * (rya[t, 1] + DT * sye[t, 0])
        flat_e[line(0, 0, 0), :] -= W[0, 0] * hz
        flat_e[line(2, 0, 0), :] += W[2, 0] * hx

    def correct_first(t):
        corner = at_row(rce[t, 0:1], ny - 1, rxa[t, 0])
        hy = flag_x * (rxa[t, 0] + DT * sxe[t, 1])
        hz = flag_x * (rxa[t, 1] - DT * (sxe[t, 0] - corner))
        E[1, 0, 0:ny] += C[5, 0] * hz
        E[2, 0, 0:ny] -= C[6, 0] * hy

    def correct_last(t):
        dhy, dhz = DT * rxe[t, 1], -DT * rxe[t, 0]
        corner = at_row(DT * rca[t, 7:8], 0, dhy)
        E[0, last, 0:ny] += C[4, last] * (
            (dhz - row_prev(dhz)) - (dhy - z_prev(dhy)) + corner
        )
        E[1, last, 0:ny] -= C[5, last] * dhz
        E[2, last, 0:ny] += C[6, last] * dhy
        H[1, nx, own] += dhy
        H[2, nx, own] += dhz

    def advance(t, carry):
        lax.fori_loop(0, nx, update_h, 0, unroll=nx)
        lax.fori_loop(0, nx, update_e, 0, unroll=nx)
        more = t < STEPS - 1
        wait_arrived(t, (2, 3))
        correct_y(t)
        wait_arrived(t, (1, 4))
        correct_first(t)

        @pl.when(more)
        def _():
            stage_first(t + 1)
            send(t + 1, (5, 0))

        wait_arrived(t, (0, 5))
        correct_last(t)

        @pl.when(more)
        def _():
            stage_last(t + 1)
            send(t + 1, (4, 1))
            stage_y(t + 1)
            send(t + 1, (2, 3))

        wait_sent(t)
        return carry

    lax.fori_loop(0, STEPS, advance, 0)


def write_out(sizes, E, H, Q, e_out, h_out, p_out, sem):
    nx, ny = sizes
    pairs = []
    for comp in range(3):
        for x, wide in halves(nx):
            part = (comp, pl.ds(x, wide))
            pairs.append((E.at[comp, pl.ds(x, wide), pl.ds(0, ny)], e_out.at[part]))
            pairs.append((H.at[comp, pl.ds(x + 1, wide), pl.ds(PAD, ny)], h_out.at[part]))
            pairs.append((Q.at[part], p_out.at[part]))
    copies = [pltpu.make_async_copy(a, b, sem.at[k]) for k, (a, b) in enumerate(pairs)]
    for copy in copies:
        copy.start()
    for copy in copies:
        copy.wait()


def shards(sizes, efield, hfield, polar, material_map, via_index, fill, perm, cond, deb, relax, conf):
    nx, ny, nz = material_map.shape
    f32 = jnp.float32
    block = jax.ShapeDtypeStruct(efield.shape, f32)
    planes = [
        pltpu.VMEM((STEPS, 2, ny, nz), f32),
        pltpu.VMEM((STEPS, 2, ny, nz), f32),
        pltpu.VMEM((STEPS, 2, nx, nz), f32),
        pltpu.VMEM((STEPS, 2, nx, nz), f32),
        pltpu.VMEM((STEPS, 8, nz), f32),
        pltpu.VMEM((STEPS, 8, nz), f32),
    ]
    hbm = pl.BlockSpec(memory_space=pltpu.HBM)
    vmem = pl.BlockSpec(memory_space=pltpu.VMEM)
    padded = pltpu.VMEM((3, nx + 1, ny + PAD, nz), f32)
    state = pl.pallas_call(
        functools.partial(kernel, sizes),
        out_shape=(padded, padded, pltpu.VMEM(efield.shape, f32)),
        in_specs=[hbm] * 11,
        out_specs=(vmem, vmem, vmem),
        scratch_shapes=[
            pltpu.VMEM((nx, ny, nz), jnp.int32),
            pltpu.VMEM((nx, ny, nz), jnp.int32),
            pltpu.VMEM((nx, ny, nz), f32),
            pltpu.VMEM((7, nx, ny, nz), f32),
            pltpu.VMEM((3, 2, nx, nz), f32),
        ]
        + [pltpu.SMEM(table.shape, f32) for table in (perm, cond, deb, relax, conf.T)]
        + planes
        + planes
        + [
            pltpu.SemaphoreType.DMA((6 * len(halves(nx)) + 11,)),
            pltpu.SemaphoreType.DMA((6, STEPS)),
            pltpu.SemaphoreType.DMA((6, STEPS)),
        ],
        compiler_params=pltpu.CompilerParams(
            collective_id=0, has_side_effects=True, vmem_limit_bytes=56 * 1024 * 1024
        ),
        cost_estimate=pl.CostEstimate(
            flops=80 * STEPS * nx * ny * nz, bytes_accessed=21 * 4 * nx * ny * nz, transcendentals=0
        ),
        name="yee_steps",
    )(perm, cond, deb, relax, conf.T, efield, hfield, polar, material_map, via_index, fill)
    return pl.pallas_call(
        functools.partial(write_out, (nx, ny)),
        out_shape=(block, block, block),
        in_specs=[pl.BlockSpec(memory_space=pl.ANY)] * 3,
        out_specs=(hbm, hbm, hbm),
        scratch_shapes=[pltpu.SemaphoreType.DMA((9 * len(halves(nx)),))],
        compiler_params=pltpu.CompilerParams(vmem_limit_bytes=4 * 1024 * 1024),
        name="write_out",
    )(*state)


def solution(mesh):
    field, cell = P(None, "gx", "gy", None), P("gx", "gy", None)
    return jax.shard_map(
        functools.partial(shards, (mesh.shape["gx"], mesh.shape["gy"])),
        mesh=mesh,
        in_specs=(field, field, field, cell, cell, cell, P(), P(), P(), P(), P()),
        out_specs=(field, field, field),
        check_vma=False,
    )
```

```python
import functools

import jax
import jax.numpy as jnp
from jax import lax
from jax.experimental import pallas as pl
from jax.experimental.pallas import tpu as pltpu
from jax.sharding import PartitionSpec as P

STEPS = 4
DT = 0.55
PAD = 8
MESH = pl.DeviceIdType.MESH


def halves(count):
    half = (count + 1) // 2
    return [(0, half), (half, count - half)] if count > 1 else [(0, count)]


def z_next(value):
    lanes = value.shape[1]
    lane = lax.broadcasted_iota(jnp.int32, value.shape, 1)
    return jnp.where(lane < lanes - 1, pltpu.roll(value, lanes - 1, 1), 0.0)


def z_prev(value):
    lane = lax.broadcasted_iota(jnp.int32, value.shape, 1)
    return jnp.where(lane > 0, pltpu.roll(value, 1, 1), 0.0)


def row_prev(value):
    row = lax.broadcasted_iota(jnp.int32, value.shape, 0)
    return jnp.where(row > 0, pltpu.roll(value, 1, 0), 0.0)


def at_row(line, row, like):
    rows = lax.broadcasted_iota(jnp.int32, like.shape, 0)
    return jnp.where(rows == row, jnp.broadcast_to(line, like.shape), 0.0)


def kernel(
    sizes,
    perm_in, cond_in, deb_in, relax_in, conf_in,
    e_in, h_in, p_in, m_in, v_in, f_in,
    E, H, Q,
    M, V, F, C, W,
    perm, cond, deb, relax, conf,
    sxe, sxa, sye, sya, sce, sca,
    rxe, rxa, rye, rya, rce, rca,
    in_sem, send_sem, recv_sem,
):
    count_x, count_y = sizes
    nx, ny, nz = m_in.shape
    mats, vias = perm.shape[0], conf.shape[1]
    gx, gy = lax.axis_index("gx"), lax.axis_index("gy")
    own = pl.ds(PAD, ny)
    last = nx - 1
    end = PAD + ny - 1

    height = ny + PAD
    flat_e = E.reshape(3 * (nx + 1) * height, nz)
    flat_h = H.reshape(3 * (nx + 1) * height, nz)

    def line(comp, x, row):
        return pl.ds((comp * (nx + 1) + x) * height + row, nx, stride=height)

    def loads():
        fields = []
        for comp in range(3):
            for x, wide in halves(nx):
                part = (comp, pl.ds(x, wide))
                fields.append((e_in.at[part], E.at[comp, pl.ds(x, wide), pl.ds(0, ny)]))
                fields.append((h_in.at[part], H.at[comp, pl.ds(x + 1, wide), own]))
        tables = [(perm_in, perm), (cond_in, cond), (deb_in, deb), (relax_in, relax), (conf_in, conf)]
        cells = [(m_in, M), (v_in, V), (f_in, F)]
        pols = [(p_in.at[comp], Q.at[comp]) for comp in range(3)]
        pairs = fields + tables + cells + pols
        copies = [pltpu.make_async_copy(a, b, in_sem.at[k]) for k, (a, b) in enumerate(pairs)]
        cut = len(fields)
        end_cells = cut + len(tables) + len(cells)
        return copies[:cut], copies[cut:end_cells], copies[end_cells:]

    low_x, high_x = gx > 0, gx < count_x - 1
    low_y, high_y = gy > 0, gy < count_y - 1
    routes = [
        ((gx - 1, gy), low_x, sxe, rxe, high_x),
        ((gx + 1, gy), high_x, sxa, rxa, low_x),
        ((gx, gy - 1), low_y, sye, rye, high_y),
        ((gx, gy + 1), high_y, sya, rya, low_y),
        ((gx + 1, gy - 1), high_x & low_y, sce, rce, low_x & high_y),
        ((gx - 1, gy + 1), low_x & high_y, sca, rca, high_x & low_y),
    ]

    barrier = pltpu.get_barrier_semaphore()
    for target, there, _, _, _ in routes:
        @pl.when(there)
        def _(target=target):
            pl.semaphore_signal(barrier, inc=1, device_id=target, device_id_type=MESH)

    first, second, third = loads()
    for copy in first[0::2] + first[1::2]:
        copy.start()

    def remote(k, t):
        target, _, source, dest, _ = routes[k]
        return pltpu.make_async_remote_copy(
            src_ref=source.at[t],
            dst_ref=dest.at[t],
            send_sem=send_sem.at[k, t],
            recv_sem=recv_sem.at[k, t],
            device_id=target,
            device_id_type=MESH,
        )

    def each(chosen, which, act):
        for k in chosen:
            @pl.when(routes[k][which])
            def _(k=k):
                act(k)

    def send(t, chosen):
        each(chosen, 1, lambda k: remote(k, t).start())

    def wait_sent(t):
        each(range(6), 1, lambda k: remote(k, t).wait_send())

    def wait_arrived(t, chosen):
        each(chosen, 4, lambda k: remote(k, t).wait_recv())

    for _, _, _, dest, sender in routes:
        @pl.when(jnp.logical_not(sender))
        def _(dest=dest):
            dest[...] = jnp.zeros(dest.shape, jnp.float32)

    for comp in range(3):
        E[comp, nx] = jnp.zeros((ny + PAD, nz), jnp.float32)
        H[comp, 0] = jnp.zeros((ny + PAD, nz), jnp.float32)
        for x in range(nx):
            E[comp, x, ny : ny + PAD] = jnp.zeros((PAD, nz), jnp.float32)
            H[comp, x + 1, 0:PAD] = jnp.zeros((PAD, nz), jnp.float32)

    def stage_first(t):
        sca[t] = E[1, 0, ny - 8 : ny]
        sxe[t] = E[1:3, 0, 0:ny]

    def stage_last(t):
        sce[t] = E[0, last, 0:8]
        ex = E[0, last, 0:ny]
        sxa[t, 0] = H[1, nx, own] - DT * (z_next(ex) - ex + E[2, last, 0:ny])
        sxa[t, 1] = H[2, nx, own] + DT * (E[1, last, 0:ny] + E[0, last, 1 : ny + 1] - ex)

    def stage_y(t):
        sye[t, 0] = flat_e[line(0, 0, 0), :]
        sye[t, 1] = flat_e[line(2, 0, 0), :]
        ey = flat_e[line(1, 0, ny - 1), :]
        sya[t, 0] = flat_h[line(0, 1, end), :] + DT * (flat_e[line(2, 0, ny - 1), :] + z_next(ey) - ey)
        sya[t, 1] = flat_h[line(2, 1, end), :] - DT * (
            flat_e[line(1, 1, ny - 1), :] - ey + flat_e[line(0, 0, ny - 1), :]
        )

    for copy in first[0::2]:
        copy.wait()
    stage_first(0)
    pl.semaphore_wait(barrier, sum(jnp.where(route[1], 1, 0) for route in routes))
    send(0, (5, 0))
    for copy in first[1::2]:
        copy.wait()
    for copy in second + third:
        copy.start()
    stage_last(0)
    send(0, (4, 1))
    stage_y(0)
    send(0, (2, 3))

    for copy in second:
        copy.wait()
    shape = (ny, nz)
    mat_eps = [jnp.full(shape, perm[m], jnp.float32) for m in range(mats)]
    mat_loss = [jnp.full(shape, cond[m] * (0.5 * DT), jnp.float32) for m in range(mats)]
    mat_kp, mat_bp = [], []
    for m in range(mats):
        tau = jnp.full(shape, 2.0 * relax[m], jnp.float32)
        mat_kp.append((tau - DT) / (tau + DT))
        mat_bp.append(jnp.full(shape, 2.0 * DT * deb[m], jnp.float32) / (tau + DT))

    def pick(ids, table):
        value = table[-1]
        for entry in range(len(table) - 2, -1, -1):
            value = jnp.where(ids == entry, table[entry], value)
        return value

    def coefficients(x, carry):
        ids, rows = M[x], V[x]
        eps = pick(ids, mat_eps) * (1.0 + F[x])
        loss = pick(ids, mat_loss)
        kp, bp = pick(ids, mat_kp), pick(ids, mat_bp)
        inv = 1.0 / (eps + loss)
        C[0, x] = (eps - loss - bp) * inv
        C[1, x] = (1.0 - kp) * inv
        C[2, x] = kp
        C[3, x] = bp
        inv = inv * DT
        for comp in range(3):
            C[4 + comp, x] = inv * pick(rows, [conf[comp, row] for row in range(vias)])
        return carry

    lax.fori_loop(0, nx, coefficients, 0, unroll=4)
    for comp in range(3):
        W[comp, 0] = C[4 + comp, :, 0, :]
        W[comp, 1] = C[4 + comp, :, ny - 1, :]
    for copy in third:
        copy.wait()

    flag_x = jnp.where(low_x, 1.0, 0.0)
    flag_y = jnp.where(low_y, 1.0, 0.0)

    def update_h(x, carry):
        ex, ey, ez = E[0, x, 0:ny], E[1, x, 0:ny], E[2, x, 0:ny]
        ex_y, ez_y = E[0, x, 1 : ny + 1], E[2, x, 1 : ny + 1]
        ey_x, ez_x = E[1, x + 1, 0:ny], E[2, x + 1, 0:ny]
        H[0, x + 1, own] = H[0, x + 1, own] - DT * ((ez_y - ez) - (z_next(ey) - ey))
        H[1, x + 1, own] = H[1, x + 1, own] - DT * ((z_next(ex) - ex) - (ez_x - ez))
        H[2, x + 1, own] = H[2, x + 1, own] - DT * ((ey_x - ey) - (ex_y - ex))
        return carry

    def update_e(x, carry):
        hx, hy, hz = H[0, x + 1, own], H[1, x + 1, own], H[2, x + 1, own]
        below = pl.ds(PAD - 1, ny)
        cx = (hz - H[2, x + 1, below]) - (hy - z_prev(hy))
        cy = (hx - z_prev(hx)) - (hz - H[2, x, own])
        cz = (hy - H[1, x, own]) - (hx - H[0, x + 1, below])
        c1, c2, kp, bp = C[0, x], C[1, x], C[2, x], C[3, x]
        for comp, curl in enumerate((cx, cy, cz)):
            value, pol = E[comp, x, 0:ny], Q[comp, x]
            E[comp, x, 0:ny] = c1 * value + c2 * pol + C[4 + comp, x] * curl
            Q[comp, x] = kp * pol + bp * value
        return carry

    def correct_y(t):
        dhx, dhz = -DT * rye[t, 1], DT * rye[t, 0]
        flat_h[line(0, 1, end), :] += dhx
        flat_h[line(2, 1, end), :] += dhz
        flat_e[line(0, 0, ny - 1), :] += W[0, 1] * dhz
        flat_e[line(1, 0, ny - 1), :] += W[1, 1] * ((dhx - z_prev(dhx)) - (dhz - row_prev(dhz)))
        flat_e[line(2, 0, ny - 1), :] -= W[2, 1] * dhx
        hx = flag_y * (rya[t, 0] - DT * sye[t, 1])
        hz = flag_y * (rya[t, 1] + DT * sye[t, 0])
        flat_e[line(0, 0, 0), :] -= W[0, 0] * hz
        flat_e[line(2, 0, 0), :] += W[2, 0] * hx

    def correct_first(t):
        corner = at_row(rce[t, 0:1], ny - 1, rxa[t, 0])
        hy = flag_x * (rxa[t, 0] + DT * sxe[t, 1])
        hz = flag_x * (rxa[t, 1] - DT * (sxe[t, 0] - corner))
        E[1, 0, 0:ny] += C[5, 0] * hz
        E[2, 0, 0:ny] -= C[6, 0] * hy

    def correct_last(t):
        dhy, dhz = DT * rxe[t, 1], -DT * rxe[t, 0]
        corner = at_row(DT * rca[t, 7:8], 0, dhy)
        E[0, last, 0:ny] += C[4, last] * (
            (dhz - row_prev(dhz)) - (dhy - z_prev(dhy)) + corner
        )
        E[1, last, 0:ny] -= C[5, last] * dhz
        E[2, last, 0:ny] += C[6, last] * dhy
        H[1, nx, own] += dhy
        H[2, nx, own] += dhz

    def advance(t, carry):
        lax.fori_loop(0, nx, update_h, 0, unroll=nx)
        lax.fori_loop(0, nx, update_e, 0, unroll=nx)
        more = t < STEPS - 1
        wait_arrived(t, (2, 3))
        correct_y(t)
        wait_arrived(t, (1, 4))
        correct_first(t)

        @pl.when(more)
        def _():
            stage_first(t + 1)
            send(t + 1, (5, 0))

        wait_arrived(t, (0, 5))
        correct_last(t)

        @pl.when(more)
        def _():
            stage_last(t + 1)
            send(t + 1, (4, 1))
            stage_y(t + 1)
            send(t + 1, (2, 3))

        wait_sent(t)
        return carry

    lax.fori_loop(0, STEPS, advance, 0)


def write_out(sizes, E, H, Q, e_out, h_out, p_out, sem):
    nx, ny = sizes
    pairs = []
    for comp in range(3):
        for x, wide in halves(nx):
            part = (comp, pl.ds(x, wide))
            pairs.append((E.at[comp, pl.ds(x, wide), pl.ds(0, ny)], e_out.at[part]))
            pairs.append((H.at[comp, pl.ds(x + 1, wide), pl.ds(PAD, ny)], h_out.at[part]))
            pairs.append((Q.at[part], p_out.at[part]))
    copies = [pltpu.make_async_copy(a, b, sem.at[k]) for k, (a, b) in enumerate(pairs)]
    for copy in copies:
        copy.start()
    for copy in copies:
        copy.wait()


def shards(sizes, efield, hfield, polar, material_map, via_index, fill, perm, cond, deb, relax, conf):
    nx, ny, nz = material_map.shape
    f32 = jnp.float32
    block = jax.ShapeDtypeStruct(efield.shape, f32)
    planes = [
        pltpu.VMEM((STEPS, 2, ny, nz), f32),
        pltpu.VMEM((STEPS, 2, ny, nz), f32),
        pltpu.VMEM((STEPS, 2, nx, nz), f32),
        pltpu.VMEM((STEPS, 2, nx, nz), f32),
        pltpu.VMEM((STEPS, 8, nz), f32),
        pltpu.VMEM((STEPS, 8, nz), f32),
    ]
    hbm = pl.BlockSpec(memory_space=pltpu.HBM)
    vmem = pl.BlockSpec(memory_space=pltpu.VMEM)
    padded = pltpu.VMEM((3, nx + 1, ny + PAD, nz), f32)
    state = pl.pallas_call(
        functools.partial(kernel, sizes),
        out_shape=(padded, padded, pltpu.VMEM(efield.shape, f32)),
        in_specs=[hbm] * 11,
        out_specs=(vmem, vmem, vmem),
        scratch_shapes=[
            pltpu.VMEM((nx, ny, nz), jnp.int32),
            pltpu.VMEM((nx, ny, nz), jnp.int32),
            pltpu.VMEM((nx, ny, nz), f32),
            pltpu.VMEM((7, nx, ny, nz), f32),
            pltpu.VMEM((3, 2, nx, nz), f32),
        ]
        + [pltpu.SMEM(table.shape, f32) for table in (perm, cond, deb, relax, conf.T)]
        + planes
        + planes
        + [
            pltpu.SemaphoreType.DMA((6 * len(halves(nx)) + 11,)),
            pltpu.SemaphoreType.DMA((6, STEPS)),
            pltpu.SemaphoreType.DMA((6, STEPS)),
        ],
        compiler_params=pltpu.CompilerParams(
            collective_id=0, has_side_effects=True, vmem_limit_bytes=56 * 1024 * 1024
        ),
        cost_estimate=pl.CostEstimate(
            flops=80 * STEPS * nx * ny * nz, bytes_accessed=21 * 4 * nx * ny * nz, transcendentals=0
        ),
        name="yee_steps",
    )(perm, cond, deb, relax, conf.T, efield, hfield, polar, material_map, via_index, fill)
    return pl.pallas_call(
        functools.partial(write_out, (nx, ny)),
        out_shape=(block, block, block),
        in_specs=[pl.BlockSpec(memory_space=pl.ANY)] * 3,
        out_specs=(hbm, hbm, hbm),
        scratch_shapes=[pltpu.SemaphoreType.DMA((9 * len(halves(nx)),))],
        compiler_params=pltpu.CompilerParams(vmem_limit_bytes=4 * 1024 * 1024),
        name="write_out",
    )(*state)


def solution(mesh):
    field, cell = P(None, "gx", "gy", None), P("gx", "gy", None)
    return jax.shard_map(
        functools.partial(shards, (mesh.shape["gx"], mesh.shape["gy"])),
        mesh=mesh,
        in_specs=(field, field, field, cell, cell, cell, P(), P(), P(), P(), P()),
        out_specs=(field, field, field),
        check_vma=False,
    )
```

```python
import functools

import jax
import jax.numpy as jnp
from jax import lax
from jax.experimental import pallas as pl
from jax.experimental.pallas import tpu as pltpu
from jax.sharding import PartitionSpec as P

STEPS = 4
DT = 0.55
PAD = 8
MESH = pl.DeviceIdType.MESH


def halves(count):
    half = (count + 1) // 2
    return [(0, half), (half, count - half)] if count > 1 else [(0, count)]


def z_next(value):
    lanes = value.shape[1]
    lane = lax.broadcasted_iota(jnp.int32, value.shape, 1)
    return jnp.where(lane < lanes - 1, pltpu.roll(value, lanes - 1, 1), 0.0)


def z_prev(value):
    lane = lax.broadcasted_iota(jnp.int32, value.shape, 1)
    return jnp.where(lane > 0, pltpu.roll(value, 1, 1), 0.0)


def row_prev(value):
    row = lax.broadcasted_iota(jnp.int32, value.shape, 0)
    return jnp.where(row > 0, pltpu.roll(value, 1, 0), 0.0)


def at_row(line, row, like):
    rows = lax.broadcasted_iota(jnp.int32, like.shape, 0)
    return jnp.where(rows == row, jnp.broadcast_to(line, like.shape), 0.0)


def kernel(
    sizes,
    perm_in, cond_in, deb_in, relax_in, conf_in,
    e_in, h_in, p_in, m_in, v_in, f_in,
    E, H, Q,
    M, V, F, C, W,
    perm, cond, deb, relax, conf,
    sxe, sxa, sye, sya, sce, sca,
    rxe, rxa, rye, rya, rce, rca,
    in_sem, send_sem, recv_sem,
):
    count_x, count_y = sizes
    nx, ny, nz = m_in.shape
    mats, vias = perm.shape[0], conf.shape[1]
    gx, gy = lax.axis_index("gx"), lax.axis_index("gy")
    own = pl.ds(PAD, ny)
    last = nx - 1
    end = PAD + ny - 1

    height = ny + PAD
    flat_e = E.reshape(3 * (nx + 1) * height, nz)
    flat_h = H.reshape(3 * (nx + 1) * height, nz)

    def line(comp, x, row):
        return pl.ds((comp * (nx + 1) + x) * height + row, nx, stride=height)

    def loads():
        fields = []
        for comp in range(3):
            for x, wide in halves(nx):
                part = (comp, pl.ds(x, wide))
                fields.append((e_in.at[part], E.at[comp, pl.ds(x, wide), pl.ds(0, ny)]))
                fields.append((h_in.at[part], H.at[comp, pl.ds(x + 1, wide), own]))
        tables = [(perm_in, perm), (cond_in, cond), (deb_in, deb), (relax_in, relax), (conf_in, conf)]
        cells = [(m_in, M), (v_in, V), (f_in, F)]
        pols = [(p_in.at[comp], Q.at[comp]) for comp in range(3)]
        pairs = fields + tables + cells + pols
        copies = [pltpu.make_async_copy(a, b, in_sem.at[k]) for k, (a, b) in enumerate(pairs)]
        cut = len(fields)
        end_cells = cut + len(tables) + len(cells)
        return copies[:cut], copies[cut:end_cells], copies[end_cells:]

    low_x, high_x = gx > 0, gx < count_x - 1
    low_y, high_y = gy > 0, gy < count_y - 1
    routes = [
        ((gx - 1, gy), low_x, sxe, rxe, high_x),
        ((gx + 1, gy), high_x, sxa, rxa, low_x),
        ((gx, gy - 1), low_y, sye, rye, high_y),
        ((gx, gy + 1), high_y, sya, rya, low_y),
        ((gx + 1, gy - 1), high_x & low_y, sce, rce, low_x & high_y),
        ((gx - 1, gy + 1), low_x & high_y, sca, rca, high_x & low_y),
    ]

    barrier = pltpu.get_barrier_semaphore()
    for target, there, _, _, _ in routes:
        @pl.when(there)
        def _(target=target):
            pl.semaphore_signal(barrier, inc=1, device_id=target, device_id_type=MESH)

    first, second, third = loads()
    for copy in first + second + third:
        copy.start()

    def remote(k, t):
        target, _, source, dest, _ = routes[k]
        return pltpu.make_async_remote_copy(
            src_ref=source.at[t],
            dst_ref=dest.at[t],
            send_sem=send_sem.at[k, t],
            recv_sem=recv_sem.at[k, t],
            device_id=target,
            device_id_type=MESH,
        )

    def each(chosen, which, act):
        for k in chosen:
            @pl.when(routes[k][which])
            def _(k=k):
                act(k)

    def send(t, chosen):
        each(chosen, 1, lambda k: remote(k, t).start())

    def wait_sent(t):
        each(range(6), 1, lambda k: remote(k, t).wait_send())

    def wait_arrived(t, chosen):
        each(chosen, 4, lambda k: remote(k, t).wait_recv())

    for _, _, _, dest, sender in routes:
        @pl.when(jnp.logical_not(sender))
        def _(dest=dest):
            dest[...] = jnp.zeros(dest.shape, jnp.float32)

    for comp in range(3):
        E[comp, nx] = jnp.zeros((ny + PAD, nz), jnp.float32)
        H[comp, 0] = jnp.zeros((ny + PAD, nz), jnp.float32)
        for x in range(nx):
            E[comp, x, ny : ny + PAD] = jnp.zeros((PAD, nz), jnp.float32)
            H[comp, x + 1, 0:PAD] = jnp.zeros((PAD, nz), jnp.float32)

    def stage_first(t):
        sca[t] = E[1, 0, ny - 8 : ny]
        sxe[t] = E[1:3, 0, 0:ny]

    def stage_last(t):
        sce[t] = E[0, last, 0:8]
        ex = E[0, last, 0:ny]
        sxa[t, 0] = H[1, nx, own] - DT * (z_next(ex) - ex + E[2, last, 0:ny])
        sxa[t, 1] = H[2, nx, own] + DT * (E[1, last, 0:ny] + E[0, last, 1 : ny + 1] - ex)

    def stage_y(t):
        sye[t, 0] = flat_e[line(0, 0, 0), :]
        sye[t, 1] = flat_e[line(2, 0, 0), :]
        ey = flat_e[line(1, 0, ny - 1), :]
        sya[t, 0] = flat_h[line(0, 1, end), :] + DT * (flat_e[line(2, 0, ny - 1), :] + z_next(ey) - ey)
        sya[t, 1] = flat_h[line(2, 1, end), :] - DT * (
            flat_e[line(1, 1, ny - 1), :] - ey + flat_e[line(0, 0, ny - 1), :]
        )

    for copy in first:
        copy.wait()
    pl.semaphore_wait(barrier, sum(jnp.where(route[1], 1, 0) for route in routes))
    stage_first(0)
    send(0, (5, 0))
    stage_last(0)
    send(0, (4, 1))
    stage_y(0)
    send(0, (2, 3))

    for copy in second:
        copy.wait()
    shape = (ny, nz)
    mat_eps = [jnp.full(shape, perm[m], jnp.float32) for m in range(mats)]
    mat_loss = [jnp.full(shape, cond[m] * (0.5 * DT), jnp.float32) for m in range(mats)]
    mat_kp, mat_bp = [], []
    for m in range(mats):
        tau = jnp.full(shape, 2.0 * relax[m], jnp.float32)
        mat_kp.append((tau - DT) / (tau + DT))
        mat_bp.append(jnp.full(shape, 2.0 * DT * deb[m], jnp.float32) / (tau + DT))

    def pick(ids, table):
        value = table[-1]
        for entry in range(len(table) - 2, -1, -1):
            value = jnp.where(ids == entry, table[entry], value)
        return value

    def coefficients(x, carry):
        ids, rows = M[x], V[x]
        eps = pick(ids, mat_eps) * (1.0 + F[x])
        loss = pick(ids, mat_loss)
        kp, bp = pick(ids, mat_kp), pick(ids, mat_bp)
        inv = 1.0 / (eps + loss)
        C[0, x] = (eps - loss - bp) * inv
        C[1, x] = (1.0 - kp) * inv
        C[2, x] = kp
        C[3, x] = bp
        inv = inv * DT
        for comp in range(3):
            C[4 + comp, x] = inv * pick(rows, [conf[comp, row] for row in range(vias)])
        return carry

    lax.fori_loop(0, nx, coefficients, 0, unroll=4)
    for comp in range(3):
        W[comp, 0] = C[4 + comp, :, 0, :]
        W[comp, 1] = C[4 + comp, :, ny - 1, :]
    for copy in third:
        copy.wait()

    flag_x = jnp.where(low_x, 1.0, 0.0)
    flag_y = jnp.where(low_y, 1.0, 0.0)

    def update_h(x, carry):
        ex, ey, ez = E[0, x, 0:ny], E[1, x, 0:ny], E[2, x, 0:ny]
        ex_y, ez_y = E[0, x, 1 : ny + 1], E[2, x, 1 : ny + 1]
        ey_x, ez_x = E[1, x + 1, 0:ny], E[2, x + 1, 0:ny]
        H[0, x + 1, own] = H[0, x + 1, own] - DT * ((ez_y - ez) - (z_next(ey) - ey))
        H[1, x + 1, own] = H[1, x + 1, own] - DT * ((z_next(ex) - ex) - (ez_x - ez))
        H[2, x + 1, own] = H[2, x + 1, own] - DT * ((ey_x - ey) - (ex_y - ex))
        return carry

    def update_e(x, carry):
        hx, hy, hz = H[0, x + 1, own], H[1, x + 1, own], H[2, x + 1, own]
        below = pl.ds(PAD - 1, ny)
        cx = (hz - H[2, x + 1, below]) - (hy - z_prev(hy))
        cy = (hx - z_prev(hx)) - (hz - H[2, x, own])
        cz = (hy - H[1, x, own]) - (hx - H[0, x + 1, below])
        c1, c2, kp, bp = C[0, x], C[1, x], C[2, x], C[3, x]
        for comp, curl in enumerate((cx, cy, cz)):
            value, pol = E[comp, x, 0:ny], Q[comp, x]
            E[comp, x, 0:ny] = c1 * value + c2 * pol + C[4 + comp, x] * curl
            Q[comp, x] = kp * pol + bp * value
        return carry

    def correct_y(t):
        dhx, dhz = -DT * rye[t, 1], DT * rye[t, 0]
        flat_h[line(0, 1, end), :] += dhx
        flat_h[line(2, 1, end), :] += dhz
        flat_e[line(0, 0, ny - 1), :] += W[0, 1] * dhz
        flat_e[line(1, 0, ny - 1), :] += W[1, 1] * ((dhx - z_prev(dhx)) - (dhz - row_prev(dhz)))
        flat_e[line(2, 0, ny - 1), :] -= W[2, 1] * dhx
        hx = flag_y * (rya[t, 0] - DT * sye[t, 1])
        hz = flag_y * (rya[t, 1] + DT * sye[t, 0])
        flat_e[line(0, 0, 0), :] -= W[0, 0] * hz
        flat_e[line(2, 0, 0), :] += W[2, 0] * hx

    def correct_first(t):
        corner = at_row(rce[t, 0:1], ny - 1, rxa[t, 0])
        hy = flag_x * (rxa[t, 0] + DT * sxe[t, 1])
        hz = flag_x * (rxa[t, 1] - DT * (sxe[t, 0] - corner))
        E[1, 0, 0:ny] += C[5, 0] * hz
        E[2, 0, 0:ny] -= C[6, 0] * hy

    def correct_last(t):
        dhy, dhz = DT * rxe[t, 1], -DT * rxe[t, 0]
        corner = at_row(DT * rca[t, 7:8], 0, dhy)
        E[0, last, 0:ny] += C[4, last] * (
            (dhz - row_prev(dhz)) - (dhy - z_prev(dhy)) + corner
        )
        E[1, last, 0:ny] -= C[5, last] * dhz
        E[2, last, 0:ny] += C[6, last] * dhy
        H[1, nx, own] += dhy
        H[2, nx, own] += dhz

    def advance(t, carry):
        lax.fori_loop(0, nx, update_h, 0, unroll=4)
        lax.fori_loop(0, nx, update_e, 0, unroll=4)
        more = t < STEPS - 1
        wait_arrived(t, (2, 3))
        correct_y(t)
        wait_arrived(t, (1, 4))
        correct_first(t)

        @pl.when(more)
        def _():
            stage_first(t + 1)
            send(t + 1, (5, 0))

        wait_arrived(t, (0, 5))
        correct_last(t)

        @pl.when(more)
        def _():
            stage_last(t + 1)
            send(t + 1, (4, 1))
            stage_y(t + 1)
            send(t + 1, (2, 3))

        wait_sent(t)
        return carry

    lax.fori_loop(0, STEPS, advance, 0)


def write_out(sizes, E, H, Q, e_out, h_out, p_out, sem):
    nx, ny = sizes
    pairs = []
    for comp in range(3):
        for x, wide in halves(nx):
            part = (comp, pl.ds(x, wide))
            pairs.append((E.at[comp, pl.ds(x, wide), pl.ds(0, ny)], e_out.at[part]))
            pairs.append((H.at[comp, pl.ds(x + 1, wide), pl.ds(PAD, ny)], h_out.at[part]))
            pairs.append((Q.at[part], p_out.at[part]))
    copies = [pltpu.make_async_copy(a, b, sem.at[k]) for k, (a, b) in enumerate(pairs)]
    for copy in copies:
        copy.start()
    for copy in copies:
        copy.wait()


def shards(sizes, efield, hfield, polar, material_map, via_index, fill, perm, cond, deb, relax, conf):
    nx, ny, nz = material_map.shape
    f32 = jnp.float32
    block = jax.ShapeDtypeStruct(efield.shape, f32)
    planes = [
        pltpu.VMEM((STEPS, 2, ny, nz), f32),
        pltpu.VMEM((STEPS, 2, ny, nz), f32),
        pltpu.VMEM((STEPS, 2, nx, nz), f32),
        pltpu.VMEM((STEPS, 2, nx, nz), f32),
        pltpu.VMEM((STEPS, 8, nz), f32),
        pltpu.VMEM((STEPS, 8, nz), f32),
    ]
    hbm = pl.BlockSpec(memory_space=pltpu.HBM)
    vmem = pl.BlockSpec(memory_space=pltpu.VMEM)
    padded = pltpu.VMEM((3, nx + 1, ny + PAD, nz), f32)
    state = pl.pallas_call(
        functools.partial(kernel, sizes),
        out_shape=(padded, padded, pltpu.VMEM(efield.shape, f32)),
        in_specs=[hbm] * 11,
        out_specs=(vmem, vmem, vmem),
        scratch_shapes=[
            pltpu.VMEM((nx, ny, nz), jnp.int32),
            pltpu.VMEM((nx, ny, nz), jnp.int32),
            pltpu.VMEM((nx, ny, nz), f32),
            pltpu.VMEM((7, nx, ny, nz), f32),
            pltpu.VMEM((3, 2, nx, nz), f32),
        ]
        + [pltpu.SMEM(table.shape, f32) for table in (perm, cond, deb, relax, conf.T)]
        + planes
        + planes
        + [
            pltpu.SemaphoreType.DMA((6 * len(halves(nx)) + 11,)),
            pltpu.SemaphoreType.DMA((6, STEPS)),
            pltpu.SemaphoreType.DMA((6, STEPS)),
        ],
        compiler_params=pltpu.CompilerParams(
            collective_id=0, has_side_effects=True, vmem_limit_bytes=56 * 1024 * 1024
        ),
        cost_estimate=pl.CostEstimate(
            flops=80 * STEPS * nx * ny * nz, bytes_accessed=21 * 4 * nx * ny * nz, transcendentals=0
        ),
        name="yee_steps",
    )(perm, cond, deb, relax, conf.T, efield, hfield, polar, material_map, via_index, fill)
    return pl.pallas_call(
        functools.partial(write_out, (nx, ny)),
        out_shape=(block, block, block),
        in_specs=[pl.BlockSpec(memory_space=pl.ANY)] * 3,
        out_specs=(hbm, hbm, hbm),
        scratch_shapes=[pltpu.SemaphoreType.DMA((9 * len(halves(nx)),))],
        compiler_params=pltpu.CompilerParams(vmem_limit_bytes=4 * 1024 * 1024),
        name="write_out",
    )(*state)


def solution(mesh):
    field, cell = P(None, "gx", "gy", None), P("gx", "gy", None)
    return jax.shard_map(
        functools.partial(shards, (mesh.shape["gx"], mesh.shape["gy"])),
        mesh=mesh,
        in_specs=(field, field, field, cell, cell, cell, P(), P(), P(), P(), P()),
        out_specs=(field, field, field),
        check_vma=False,
    )
```
